128 devices in a mesh: gx: 16 (over y, z_hi, core), gy: 8 (over x, z_lo).
Axes of the slice: x: 4, y: 4, z: 4 (z_hi: 2, z_lo: 2; z = z_hi * 2 + z_lo), core: 2. Of those that a mesh axis runs over, the one named last changes fastest.
Arguments:
- magnetic: float32 [3, 32, 512, 4096], P(None, None, 'gy', 'gx'), may hold values from -6 to 6
- register: float32 [3, 32, 512, 4096], P(None, None, 'gy', 'gx'), may hold values from -1.2 to 1.2
- velocity: float32 [3, 8, 128, 1024], P(None, 'gy', 'gx'), may hold values from -6 to 6
- prolong_taps: float32 [3, 4, 3], replicated, may hold values from 0 to 1, as said below
- owner_map: int32 [8], replicated, may hold values from 0 to 7, each once
Outputs:
- new_magnetic: float32 [3, 32, 512, 4096], P(None, None, 'gy', 'gx')
- new_register: float32 [3, 32, 512, 4096], P(None, None, 'gy', 'gx')
The draws below stay inside these ranges and needn't reach their ends.
Inputs may be any that keep to these rules, and one draw needn't show every extreme that they name: `owner_map`: each of 0 to 7 appears once. `prolong_taps`: along each axis, the three taps of each fine offset are positive and sum to one.
All inputs are finite; a program needn't handle non-finite values.
Results may differ from the reference program's by a relative error of at most 0.0003.
Values sent between devices are 32-bit elements; how exact they have to be, the bound alone decides.
A program may use at most 192 MiB of HBM per device.

```python
import math
import jax
import jax.numpy as jnp
from jax import lax

NZ = 32
R = 4
NX = 4096
NY = 512
KX = 1024
KY = 128
KZ = 8


def cycles_over(cells):
    return max(1, cells // 48)


def wave_table(key, cells, turns):
    phases = jax.random.uniform(key, (3, 1), jnp.float32, -math.pi, math.pi)
    steps_int = jnp.arange(cells, dtype=jnp.int32) * turns % cells
    angle = steps_int.astype(jnp.float32) * (2.0 * math.pi / cells)
    return jnp.sin(angle[None, :] + phases)


def draw_magnetic(key, part):
    key = jax.random.fold_in(key, 11)
    keys = jax.random.split(key, 4)
    wave_cols = wave_table(keys[0], NX, cycles_over(NX))
    wave_rows = wave_table(keys[1], NY, cycles_over(NY))
    wave_depth = wave_table(keys[2], NZ, 1)
    smooth = wave_cols[:, None, None, :] + wave_rows[:, None, :, None] + wave_depth[:, :, None, None]
    rough = jnp.clip(0.3 * jax.random.normal(keys[3], (3, NZ, NY, NX), jnp.float32), -1.2, 1.2)
    return 1.6 * smooth + rough


def draw_velocity(key, part):
    key = jax.random.fold_in(key, 23)
    keys = jax.random.split(key, 3)
    wave_cols = wave_table(keys[0], KX, cycles_over(NX))
    wave_rows = wave_table(keys[1], KY, cycles_over(NY))
    smooth = wave_cols[:, None, None, :] + wave_rows[:, None, :, None]
    smooth = jnp.broadcast_to(smooth, (3, KZ, KY, KX))
    rough = jnp.clip(0.3 * jax.random.normal(keys[2], (3, KZ, KY, KX), jnp.float32), -1.2, 1.2)
    return 2.2 * smooth + rough


def draw_prolong_taps(key, part):
    key = jax.random.fold_in(key, 37)
    position = (jnp.arange(R, dtype=jnp.float32) + 0.5) / R - 0.5
    linear = jnp.stack([jnp.maximum(-position, 0.0), 1.0 - jnp.abs(position), jnp.maximum(position, 0.0)], axis=1)
    jitter = jax.random.uniform(key, (3, R, 3), jnp.float32, 0.04, 0.3)
    raw_taps = linear[None, :, :] + jitter
    return raw_taps / jnp.sum(raw_taps, axis=2, keepdims=True)


def levels(rng, dims, shards, low, high):
    gain = 1.0
    for dim, shards_of in shards:
        draws = jax.random.uniform(jax.random.fold_in(jax.random.fold_in(rng, 6), dim), (shards_of,), jnp.float32, low / len(shards), high / len(shards))
        gain = gain * jnp.repeat(jnp.exp(draws), dims[dim] // shards_of).reshape((-1,) + (1,) * (len(dims) - 1 - dim))
    return gain


def bell_draw(own_key, dims, width, limit, cuts=(), held_as=jnp.bfloat16):
    array = jax.random.normal(own_key, dims, jnp.float32) * width
    if len(cuts) > 0:
        array = levels(own_key, dims, cuts, -0.22, 0.18) * array
    return jnp.clip(array, min=-limit, max=limit).astype(held_as)


def setup_inputs(seed: int = 0) -> dict:
    splits = jax.random.split(jax.random.key(seed), 6)
    return {
        "magnetic": draw_magnetic(jax.random.fold_in(splits[5], 71), 0),
        "register": bell_draw(splits[1], (3, NZ, NY, NX), 0.2, 1.2, ((2, 8), (3, 16)), jnp.float32),
        "velocity": draw_velocity(jax.random.fold_in(splits[5], 71), 0),
        "prolong_taps": draw_prolong_taps(jax.random.fold_in(splits[5], 71), 0),
        "owner_map": jax.random.permutation(splits[4], KZ).astype(jnp.int32),
    }


alpha_pade = 0.25
coef_pade = 1.5
rk_keep = -5.0 / 9.0
rk_gain = 15.0 / 16.0
reynolds = 10000.0


def prolong_axis(values_in, taps_axis, axis_pos):
    cells_in = values_in.shape[axis_pos]
    fine_count = cells_in * R
    offsets = jnp.arange(fine_count, dtype=jnp.int32) % R
    onehot = (offsets[:, None] == jnp.arange(R, dtype=jnp.int32)[None, :]).astype(values_in.dtype)
    weights = jnp.dot(onehot, taps_axis, precision=lax.Precision.HIGHEST)
    broad_shape = [1] * values_in.ndim
    broad_shape[axis_pos] = fine_count
    preceding = jnp.roll(values_in, 1, axis_pos)
    following = jnp.roll(values_in, -1, axis_pos)
    summed = jnp.repeat(preceding, R, axis=axis_pos) * weights[:, 0].reshape(broad_shape)
    summed = summed + jnp.repeat(values_in, R, axis=axis_pos) * weights[:, 1].reshape(broad_shape)
    summed = summed + jnp.repeat(following, R, axis=axis_pos) * weights[:, 2].reshape(broad_shape)
    return summed


def compact_derivative(values_in, axis_pos, spacing):
    cells_in = values_in.shape[axis_pos]
    angles = 2.0 * math.pi * jnp.arange(cells_in // 2 + 1) / cells_in
    symbol = coef_pade * jnp.sin(angles) / (spacing * (1.0 + 2.0 * alpha_pade * jnp.cos(angles)))
    broad_shape = [1] * values_in.ndim
    broad_shape[axis_pos] = cells_in // 2 + 1
    spectrum = jnp.fft.rfft(values_in, axis=axis_pos)
    result = jnp.fft.irfft(spectrum * (1j * symbol).reshape(broad_shape), n=cells_in, axis=axis_pos)
    return result.astype(values_in.dtype)


def laplacian(values_in, spacing):
    summed = -6.0 * values_in
    for axis_pos in (1, 2, 3):
        summed = summed + jnp.roll(values_in, 1, axis_pos) + jnp.roll(values_in, -1, axis_pos)
    return summed / (spacing * spacing)


def reference(magnetic, register, velocity, prolong_taps, owner_map):
    select = (owner_map[:, None] == jnp.arange(KZ, dtype=jnp.int32)[None, :]).astype(velocity.dtype)
    placed = jnp.einsum("bp,cbyx->cpyx", select, velocity, precision=lax.Precision.HIGHEST)
    fine_flow = prolong_axis(placed, prolong_taps[2], 1)
    fine_flow = prolong_axis(fine_flow, prolong_taps[1], 2)
    fine_flow = prolong_axis(fine_flow, prolong_taps[0], 3)
    spacing = 2.0 * math.pi / NX
    elec_x = fine_flow[1] * magnetic[2] - fine_flow[2] * magnetic[1]
    elec_y = fine_flow[2] * magnetic[0] - fine_flow[0] * magnetic[2]
    elec_z = fine_flow[0] * magnetic[1] - fine_flow[1] * magnetic[0]
    curl_x = compact_derivative(elec_z, 1, spacing) - compact_derivative(elec_y, 0, spacing)
    curl_y = compact_derivative(elec_x, 0, spacing) - compact_derivative(elec_z, 2, spacing)
    curl_z = compact_derivative(elec_y, 2, spacing) - compact_derivative(elec_x, 1, spacing)
    curl_field = jnp.stack([curl_x, curl_y, curl_z])
    laplace_field = laplacian(magnetic, spacing)
    diffusivity = 2.0 * math.pi / reynolds
    new_register = rk_keep * register + (0.25 * spacing) * (curl_field + diffusivity * laplace_field)
    new_magnetic = magnetic + rk_gain * new_register
    return new_magnetic, new_register
```

```python
import functools
import math

import jax
import jax.numpy as jnp
import ml_dtypes
import numpy as np
from jax import lax
from jax.experimental import pallas as pl
from jax.experimental.pallas import tpu as pltpu
from jax.sharding import PartitionSpec as P

MESH = pl.DeviceIdType.MESH
F32 = jnp.float32
BF16 = jnp.bfloat16
HIGHEST = lax.Precision.HIGHEST

R = 4
LANES = 128
ROWS = 8
TAIL = 16

alpha_pade = 0.25
coef_pade = 1.5
rk_keep = -5.0 / 9.0
rk_gain = 15.0 / 16.0
reynolds = 10000.0
decay = (-1.0 + math.sqrt(1.0 - 4.0 * alpha_pade * alpha_pade)) / (2.0 * alpha_pade)
scale = coef_pade / 2.0 * (1.0 + decay * decay)


def difference_matrix(cells):
    step = np.arange(cells)[None, :] - np.arange(cells)[:, None]
    return np.where(step == 0, 0.0, np.sign(step) * decay ** np.maximum(np.abs(step) - 1, 0))


def split_constant(matrix):
    high = matrix.astype(np.float32).astype(ml_dtypes.bfloat16)
    low = (matrix - high.astype(np.float64)).astype(np.float32).astype(ml_dtypes.bfloat16)
    return high, low


def split(value):
    high = value.astype(BF16)
    low = (value - high.astype(F32)).astype(BF16)
    return high, low


def iota(shape, dim):
    return lax.broadcasted_iota(jnp.int32, shape, dim)


def tap_weights(taps, axis, offset, neighbour):
    out = jnp.zeros(offset.shape, F32)
    for o in range(R):
        for s in range(3):
            out = jnp.where((offset == o) & (neighbour == s), taps[axis, o, s], out)
    return out


def powers(shape, dim, flip):
    index = iota(shape, dim)
    if flip:
        index = shape[dim] - 1 - index
    magnitude = jnp.exp(index.astype(F32) * math.log(abs(decay)))
    return jnp.where((index & 1) == 1, -magnitude, magnitude)


def steps(count, unroll, body, carry):
    def outer(i, carry):
        for k in range(unroll):
            carry = body(i * unroll + k, carry)
        return carry

    return lax.fori_loop(0, count // unroll, outer, carry)


def kernel(
    groups_x, groups_y, nu,
    taps, owner, mag_hbm, reg_hbm, vel_hbm, dx_hbm, dy_hbm,
    nm, nr,
    vel, sv, sh, rv, rh, bxs, bxr, bys, byr, exs, exr, eys, eyr,
    px, py, pz, xv, xh, u, ub, eh, el, dx, dy,
    in_sem, const_sem, vsend, vrecv, hsend, hrecv, bsend, brecv, esend, erecv,
):
    gx, gy = lax.axis_index("gx"), lax.axis_index("gy")
    _, depth, rows, cols = nm.shape
    planes = groups_y
    half = gx // 2
    parity = gx - 2 * half
    halo_brick = lax.rem(half + groups_y + 2 * parity - 1, groups_y)
    self_main = half == gy
    self_halo = halo_brick == gy

    vel_copy = pltpu.make_async_copy(vel_hbm, vel, const_sem.at[0])
    vel_copy.start()
    mag_copies, reg_copies = [], []
    for c in range(3):
        mag_copies.append(pltpu.make_async_copy(mag_hbm.at[c], nm.at[c], in_sem.at[c]))
        reg_copies.append(pltpu.make_async_copy(reg_hbm.at[c], nr.at[c], in_sem.at[3 + c]))
        mag_copies[c].start()
        reg_copies[c].start()
    dx_copy = pltpu.make_async_copy(dx_hbm, dx, const_sem.at[1])
    dy_copy = pltpu.make_async_copy(dy_hbm, dy, const_sem.at[2])
    dx_copy.start()
    dy_copy.start()

    barrier = pltpu.get_barrier_semaphore()
    x_low, x_high = lax.rem(gx + groups_x - 1, groups_x), lax.rem(gx + 1, groups_x)
    y_low, y_high = lax.rem(gy + groups_y - 1, groups_y), lax.rem(gy + 1, groups_y)
    sides = ((x_low, gy), (x_high, gy), (gx, y_low), (gx, y_high))

    def greet(p, _):
        for k in range(4):
            source = lax.rem(2 * gy + k - 1 + groups_x, groups_x)

            @pl.when(jnp.logical_not((source == gx) & (p == gy)))
            def _():
                pl.semaphore_signal(barrier, inc=1, device_id=(source, p), device_id_type=MESH)

        return 0

    lax.fori_loop(0, planes, greet, 0)
    for side in sides:
        pl.semaphore_signal(barrier, inc=1, device_id=side, device_id_type=MESH)

    vel_copy.wait()
    lanes8 = iota((ROWS, LANES), 1)
    row8 = iota((ROWS, LANES), 0)
    width = vel.shape[3]
    for pair in range(groups_x // 2):
        for odd in range(2):
            t = 2 * pair + odd
            halo = jnp.zeros((ROWS, LANES), F32)
            for c in range(3):
                here = vel[c, 0, :, pair * LANES : (pair + 1) * LANES]
                if odd == 0:
                    other = ((pair - 1) * LANES) % width
                    other = vel[c, 0, :, other : other + LANES]
                    block = pltpu.roll(jnp.where(lanes8 == LANES - 1, other, here), 1, 1)
                else:
                    other = ((pair + 1) * LANES) % width
                    other = vel[c, 0, :, other : other + LANES]
                    block = pltpu.roll(jnp.where(lanes8 < LANES // 4, other, here), LANES // 2 + 1, 1)
                sv[t, c] = block
                edge = jnp.where(parity == 0, block[0:1, :], block[ROWS - 1 : ROWS, :])
                halo = jnp.where(row8 == c, edge, halo)
            sh[t] = halo

    count = 2 * groups_x + 4 - jnp.where(self_main, 1, 0) - jnp.where(self_halo, 1, 0)
    pl.semaphore_wait(barrier, count)

    def send(i, _):
        t = lax.rem(gx + i, groups_x)
        for own, brick, src, dst, ssem, rsem in (
            (self_main, half, sv.at[t], rv.at[gy, parity], vsend, vrecv),
            (self_halo, halo_brick, sh.at[t], rh.at[gy, 1 - parity], hsend, hrecv),
        ):
            mine = own & (t == gx)

            @pl.when(mine)
            def _():
                pltpu.make_async_copy(src, dst, rsem).start()

            @pl.when(jnp.logical_not(mine))
            def _():
                pltpu.make_async_remote_copy(
                    src_ref=src, dst_ref=dst, send_sem=ssem, recv_sem=rsem,
                    device_id=(t, brick), device_id_type=MESH,
                ).start()

        return 0

    lax.fori_loop(0, groups_x, send, 0)

    shape = (LANES, cols)
    q, f = iota(shape, 0), iota(shape, 1)
    px[...] = tap_weights(taps, 0, f & 3, q - (f >> 2))
    shape = (rows, 4 * ROWS)
    f, q = iota(shape, 0), iota(shape, 1)
    for c in range(3):
        place = jnp.where(q == 2 * ROWS + c, -1, jnp.where(q == 3 * ROWS + c, 2 * ROWS, q))
        valid = (q < 2 * ROWS) | (q == 2 * ROWS + c) | (q == 3 * ROWS + c)
        neighbour = jnp.where(valid, place - (f >> 2) + 1, -1)
        py[c] = tap_weights(taps, 1, f & 3, neighbour)
    kz = planes * ROWS
    shape = (depth * ROWS, kz)
    f, q = iota(shape, 0), iota(shape, 1)
    owner_of = jnp.zeros(shape, jnp.int32)
    for b in range(planes):
        owner_of = jnp.where((q >> 3) == b, owner[b], owner_of)
    parent = f >> 5
    weights = jnp.zeros(shape, F32)
    for s in range(3):
        target = parent + (s - 1)
        target = jnp.where(target < 0, target + planes, jnp.where(target >= planes, target - planes, target))
        weights = weights + jnp.where(
            (owner_of == target) & ((q & 7) == (f & 7)),
            tap_weights(taps, 2, (f >> 3) & 3, jnp.full(shape, s, jnp.int32)),
            0.0,
        )
    z_high, z_low = split(weights * scale * 0.25)
    pz[0] = z_high
    pz[1] = z_low

    row_of = iota((rows, cols), 0)
    lane_of = iota((rows, cols), 1)
    edge_lane = iota((rows, LANES), 1)
    for c in range(3):
        mag_copies[c].wait()
        reg_copies[c].wait()

        def base(z, carry):
            low, high = carry
            b = nm[c, z]
            before = nm[c, lax.rem(z + depth - 1, depth)]
            after = nm[c, lax.rem(z + 1, depth)]
            total = before + after - 6.0 * b
            total = total + jnp.where(row_of == 0, 0.0, pltpu.roll(b, 1, 0))
            total = total + jnp.where(row_of == rows - 1, 0.0, pltpu.roll(b, rows - 1, 0))
            total = total + jnp.where(lane_of == 0, 0.0, pltpu.roll(b, 1, 1))
            total = total + jnp.where(lane_of == cols - 1, 0.0, pltpu.roll(b, cols - 1, 1))
            nr[c, z] = rk_keep * nr[c, z] + nu * total
            bys[0, pl.ds(c * depth + z, 1), :] = b[0:1, :]
            bys[1, pl.ds(c * depth + z, 1), :] = b[rows - 1 : rows, :]
            here = edge_lane == c * 32 + z
            low = jnp.where(here, b[:, 0:1], low)
            high = jnp.where(here, b[:, cols - 1 : cols], high)
            return low, high

        if c == 0:
            edges = (jnp.zeros((rows, LANES), F32), jnp.zeros((rows, LANES), F32))
        edges = steps(depth, 2, base, edges)
    bxs[0], bxs[1] = edges

    def exchange(xs, xr, ys, yr, ssem, rsem):
        copies = []
        for k in range(4):
            src, dst = (xs, xr) if k < 2 else (ys, yr)
            copies.append(
                pltpu.make_async_remote_copy(
                    src_ref=src.at[k % 2], dst_ref=dst.at[1 - k % 2],
                    send_sem=ssem.at[k], recv_sem=rsem.at[k],
                    device_id=sides[k], device_id_type=MESH,
                )
            )
        for copy in copies:
            copy.start()
        return copies

    b_copies = exchange(bxs, bxr, bys, byr, bsend, brecv)

    pltpu.make_async_copy(rv, rv, vrecv).wait()
    pltpu.make_async_copy(rh, rh, hrecv).wait()
    xv[...] = jnp.dot(
        rv[...].reshape(planes * 6 * ROWS, LANES), px[...], precision=HIGHEST, preferred_element_type=F32
    ).reshape(xv.shape)
    xh[...] = jnp.dot(
        rh[...].reshape(planes * 2 * ROWS, LANES), px[...], precision=HIGHEST, preferred_element_type=F32
    ).reshape(xh.shape)

    def along_y(p, _):
        for c in range(3):
            coarse = jnp.concatenate([xv[p, 0, c], xv[p, 1, c], xh[p, 0], xh[p, 1]], axis=0)
            u[c, p] = jnp.dot(py[c], coarse, precision=HIGHEST, preferred_element_type=F32)
        return 0

    lax.fori_loop(0, planes, along_y, 0)

    strip = 2 * ROWS
    lane_low = powers((1, LANES), 1, False)
    lane_high = powers((1, LANES), 1, True)
    sub_low = powers((strip, cols), 0, False)
    sub_high = powers((strip, cols), 0, True)
    strip_lane = iota((strip, LANES), 1)
    warm = TAIL if depth > TAIL else depth
    around = 1.0 if depth > TAIL else 1.0 / (1.0 - decay**depth)

    def strips(j, _):
        r0 = pl.multiple_of(j * strip, strip)
        for h in range(2):
            for c in range(3):
                coarse = u[c, :, pl.ds(pl.multiple_of(r0 + h * ROWS, ROWS), ROWS), :].reshape(kz, cols)
                high, low = split(coarse)
                fine = jnp.dot(pz[0], high, preferred_element_type=F32)
                fine = fine + jnp.dot(pz[0], low, preferred_element_type=F32)
                fine = fine + jnp.dot(pz[1], high, preferred_element_type=F32)
                ub[c, :, h * ROWS : (h + 1) * ROWS, :] = fine.reshape(depth, ROWS, cols)

        def cross(z, carry):
            low, high = carry
            us = [ub[c, z] for c in range(3)]
            bs = [nm[c, z, pl.ds(r0, strip), :] for c in range(3)]
            for c in range(3):
                a, b = (c + 1) % 3, (c + 2) % 3
                e = us[a] * bs[b] - us[b] * bs[a]
                ub[c, z] = e
                e_high, e_low = split(e)
                eh[c, z, pl.ds(r0, strip), :] = e_high
                el[c, z, pl.ds(r0, strip), :] = e_low
                if c > 0:
                    here = strip_lane == (c - 1) * 32 + z
                    sum_low = jnp.sum(e[:, :LANES] * lane_low, axis=1, keepdims=True)
                    sum_high = jnp.sum(e[:, cols - LANES :] * lane_high, axis=1, keepdims=True)
                    low = jnp.where(here, sum_low, low)
                    high = jnp.where(here, sum_high, high)
            return low, high

        zeros = jnp.zeros((strip, LANES), F32)
        low, high = steps(depth, 2, cross, (zeros, zeros))
        exs[0, pl.ds(r0, strip), :] = low
        exs[1, pl.ds(r0, strip), :] = high

        for side, at, weight in ((0, 0, sub_low), (1, rows // strip - 1, sub_high)):

            @pl.when(j == at)
            def _():
                def edge(z, _):
                    for k, c in enumerate((0, 2)):
                        total = jnp.sum(ub[c, z] * weight, axis=0, keepdims=True)
                        eys[side, pl.ds(k * depth + z, 1), :] = total
                    return 0

                steps(depth, 2, edge, 0)

        def warm_up(i, carry):
            bx, by, ax, ay = carry
            z = depth - warm + i
            bx = ub[0, z] + decay * bx
            by = ub[1, z] + decay * by
            z = warm - 1 - i
            ax = ub[0, z] + decay * ax
            ay = ub[1, z] + decay * ay
            return bx, by, ax, ay

        zeros = jnp.zeros((strip, cols), F32)
        carry = steps(warm, 2, warm_up, (zeros,) * 4)
        if around != 1.0:
            carry = tuple(around * value for value in carry)

        def along_z(i, carry):
            bx, by, ax, ay = carry
            z = i
            nr[1, z, pl.ds(r0, strip), :] += -bx
            nr[0, z, pl.ds(r0, strip), :] += by
            bx = ub[0, z] + decay * bx
            by = ub[1, z] + decay * by
            z = depth - 1 - i
            nr[1, z, pl.ds(r0, strip), :] += ax
            nr[0, z, pl.ds(r0, strip), :] += -ay
            ax = ub[0, z] + decay * ax
            ay = ub[1, z] + decay * ay
            return bx, by, ax, ay

        steps(depth, 2, along_z, carry)
        return 0

    lax.fori_loop(0, rows // strip, strips, 0)
    e_copies = exchange(exs, exr, eys, eyr, esend, erecv)
    dx_copy.wait()
    dy_copy.wait()
    for copy in b_copies + e_copies:
        copy.wait_recv()

    first_row = jnp.where(iota((ROWS, cols), 0) == 0, nu, 0.0)
    last_row = jnp.where(iota((ROWS, cols), 0) == ROWS - 1, nu, 0.0)
    first_lane = jnp.where(iota((1, LANES), 1) == 0, nu, 0.0)
    last_lane = jnp.where(iota((1, LANES), 1) == LANES - 1, nu, 0.0)

    def finish(z, _):
        highs = [eh[c, z] for c in range(3)]
        lows = [el[c, z] for c in range(3)]
        along_x = [None] * 3
        along_y = [None] * 3
        for c in (1, 2):
            along_x[c] = jnp.dot(
                jnp.concatenate([highs[c], lows[c], highs[c]], axis=1), dx[...], preferred_element_type=F32
            )
        for c in (0, 2):
            along_y[c] = jnp.dot(
                dy[...], jnp.concatenate([highs[c], lows[c], highs[c]], axis=0), preferred_element_type=F32
            )
        local = [along_y[2], -along_x[2], along_x[1] - along_y[0]]
        back = lax.rem(LANES - z, LANES)
        x_e = [pltpu.roll(exr[k], back, 1) for k in range(2)]
        x_b = [pltpu.roll(bxr[k], back, 1) for k in range(2)]
        for c in range(3):
            total = nr[c, z] + local[c]
            lo = x_b[0][:, c * 32 : c * 32 + 1] * first_lane
            hi = x_b[1][:, c * 32 : c * 32 + 1] * last_lane
            if c == 1:
                lo = lo + x_e[0][:, 32:33] * lane_low
                hi = hi - x_e[1][:, 32:33] * lane_high
            if c == 2:
                lo = lo - x_e[0][:, 0:1] * lane_low
                hi = hi + x_e[1][:, 0:1] * lane_high
            if cols == 2 * LANES:
                total = total + jnp.concatenate([lo, hi], axis=1)
            top = byr[0, pl.ds(c * depth + z, 1), :] * first_row
            bottom = byr[1, pl.ds(c * depth + z, 1), :] * last_row
            pad = jnp.zeros((ROWS, cols), F32)
            top = jnp.concatenate([top, pad], axis=0)
            bottom = jnp.concatenate([pad, bottom], axis=0)
            if c == 0:
                top = top - eyr[0, pl.ds(depth + z, 1), :] * sub_low
                bottom = bottom + eyr[1, pl.ds(depth + z, 1), :] * sub_high
            if c == 2:
                top = top + eyr[0, pl.ds(z, 1), :] * sub_low
                bottom = bottom - eyr[1, pl.ds(z, 1), :] * sub_high
            total = jnp.concatenate(
                [total[:strip] + top, total[strip : rows - strip], total[rows - strip :] + bottom], axis=0
            )
            nr[c, z] = total
            nm[c, z] = nm[c, z] + rk_gain * total
        return 0

    lax.fori_loop(0, depth, finish, 0)

    for copy in b_copies + e_copies:
        copy.wait_send()
    for own, ref, sem in ((self_main, sv, vsend), (self_halo, sh, hsend)):

        @pl.when(own)
        def _():
            part = ref.at[pl.ds(0, groups_x - 1)]
            pltpu.make_async_copy(part, part, sem).wait()

        @pl.when(jnp.logical_not(own))
        def _():
            pltpu.make_async_copy(ref, ref, sem).wait()


def body(groups_x, groups_y, magnetic, register, velocity, prolong_taps, owner_map):
    shape = magnetic.shape
    _, depth, rows, cols = shape
    planes = groups_y
    spacing = 2.0 * math.pi / (cols * groups_x)
    nu = 2.0 * math.pi / reynolds / (4.0 * spacing)
    x_high, x_low = split_constant(difference_matrix(cols).T)
    y_high, y_low = split_constant(difference_matrix(rows))
    dx = jnp.asarray(np.concatenate([x_high, x_high, x_low], axis=0))
    dy = jnp.asarray(np.concatenate([y_high, y_high, y_low], axis=1))
    brick = pltpu.VMEM(shape, F32)
    dma = pltpu.SemaphoreType.DMA
    anywhere = pl.BlockSpec(memory_space=pltpu.HBM)
    return pl.pallas_call(
        functools.partial(kernel, groups_x, groups_y, nu),
        out_shape=(brick, brick),
        in_specs=[pl.BlockSpec(memory_space=pltpu.SMEM)] * 2 + [anywhere] * 5,
        out_specs=(pl.BlockSpec(memory_space=pltpu.VMEM),) * 2,
        scratch_shapes=[
            pltpu.VMEM(velocity.shape, F32),
            pltpu.VMEM((groups_x, 3, ROWS, LANES), F32),
            pltpu.VMEM((groups_x, ROWS, LANES), F32),
            pltpu.VMEM((planes, 2, 3, ROWS, LANES), F32),
            pltpu.VMEM((planes, 2, ROWS, LANES), F32),
            pltpu.VMEM((2, rows, LANES), F32),
            pltpu.VMEM((2, rows, LANES), F32),
            pltpu.VMEM((2, 3 * depth, cols), F32),
            pltpu.VMEM((2, 3 * depth, cols), F32),
            pltpu.VMEM((2, rows, LANES), F32),
            pltpu.VMEM((2, rows, LANES), F32),
            pltpu.VMEM((2, 2 * depth, cols), F32),
            pltpu.VMEM((2, 2 * depth, cols), F32),
            pltpu.VMEM((LANES, cols), F32),
            pltpu.VMEM((3, rows, 4 * ROWS), F32),
            pltpu.VMEM((2, depth * ROWS, planes * ROWS), BF16),
            pltpu.VMEM((planes, 2, 3, ROWS, cols), F32),
            pltpu.VMEM((planes, 2, ROWS, cols), F32),
            pltpu.VMEM((3, planes, rows, cols), F32),
            pltpu.VMEM((3, depth, 2 * ROWS, cols), F32),
            pltpu.VMEM(shape, BF16),
            pltpu.VMEM(shape, BF16),
            pltpu.VMEM(dx.shape, BF16),
            pltpu.VMEM(dy.shape, BF16),
            dma((6,)), dma((3,)), dma, dma, dma, dma, dma((4,)), dma((4,)), dma((4,)), dma((4,)),
        ],
        compiler_params=pltpu.CompilerParams(
            collective_id=0, has_side_effects=True, vmem_limit_bytes=40 << 20
        ),
    )(prolong_taps, owner_map, magnetic, register, velocity, dx, dy)


def solution(mesh):
    brick = P(None, None, "gy", "gx")
    return jax.shard_map(
        functools.partial(body, mesh.shape["gx"], mesh.shape["gy"]),
        mesh=mesh,
        in_specs=(brick, brick, P(None, "gy", "gx", None), P(), P()),
        out_specs=(brick, brick),
        check_vma=False,
    )
```

```python
import functools
import math

import jax
import jax.numpy as jnp
from jax import lax
from jax.experimental import pallas as pl
from jax.experimental.pallas import tpu as pltpu
from jax.sharding import PartitionSpec as P

MESH = pl.DeviceIdType.MESH
F32 = jnp.float32
BF16 = jnp.bfloat16

R = 4
LANES = 128
ROWS = 8
UNROLL_BORDER = 8
UNROLL_BASE = 4
UNROLL_BESIDE = 4
UNROLL_CROSS = 2
UNROLL_EDGE = 8
UNROLL_Z = 8
GROUP = 8
OUT = 4
TAIL = 16

alpha_pade = 0.25
coef_pade = 1.5
rk_keep = -5.0 / 9.0
rk_gain = 15.0 / 16.0
reynolds = 10000.0
decay = (-1.0 + math.sqrt(1.0 - 4.0 * alpha_pade * alpha_pade)) / (2.0 * alpha_pade)
scale = coef_pade / 2.0 * (1.0 + decay * decay)


def split(value):
    high = value.astype(BF16)
    low = (value - high.astype(F32)).astype(BF16)
    return high, low


def iota(shape, dim):
    return lax.broadcasted_iota(jnp.int32, shape, dim)


def tap_weights(taps, axis, offset, neighbour):
    out = jnp.zeros(offset.shape, F32)
    for o in range(R):
        for s in range(3):
            out = jnp.where((offset == o) & (neighbour == s), taps[axis, o, s], out)
    return out


def powers(shape, dim, flip):
    index = iota(shape, dim)
    if flip:
        index = shape[dim] - 1 - index
    magnitude = jnp.exp(index.astype(F32) * math.log(abs(decay)))
    return jnp.where((index & 1) == 1, -magnitude, magnitude)


def steps(count, unroll, body, carry):
    def outer(i, carry):
        for k in range(unroll):
            carry = body(i * unroll + k, carry)
        return carry

    return lax.fori_loop(0, count // unroll, outer, carry)


def difference(shape, dim_source, dim_target):
    step = iota(shape, dim_source) - iota(shape, dim_target)
    size = jnp.maximum(jnp.abs(step) - 1, 0)
    magnitude = jnp.exp(size.astype(F32) * math.log(abs(decay)))
    signed = jnp.where((size & 1) == 1, -magnitude, magnitude)
    return jnp.where(step > 0, signed, jnp.where(step < 0, -signed, 0.0))


def dot(a, b):
    return jnp.dot(a, b, preferred_element_type=F32)


def kernel(
    groups_x, groups_y, nu,
    taps_hbm, owner_hbm, mag_hbm, reg_hbm, vel_hbm,
    nm, nr, exr, eyr,
    taps, owner, vel, sv, s1, hs, rv, rh, bxs, bxr, bys, byr, exs, eys,
    px, py, xc, u, ub, dx, dy,
    in_sem, const_sem, vsend, vrecv, wsend, wrecv, hsend, hrecv, bsend, brecv, esend, erecv,
):
    gx, gy = lax.axis_index("gx"), lax.axis_index("gy")
    _, depth, rows, cols = nm.shape
    planes = groups_y

    vel_copy = pltpu.make_async_copy(vel_hbm, vel, const_sem.at[0])
    vel_copy.start()
    taps_copy = pltpu.make_async_copy(taps_hbm, taps, const_sem.at[1])
    owner_copy = pltpu.make_async_copy(owner_hbm, owner, const_sem.at[2])
    taps_copy.start()
    owner_copy.start()
    mag_copies, reg_copies = [], []
    for c in range(3):
        mag_copies.append(pltpu.make_async_copy(mag_hbm.at[c], nm.at[c], in_sem.at[c]))
        reg_copies.append(pltpu.make_async_copy(reg_hbm.at[c], nr.at[c], in_sem.at[3 + c]))
        mag_copies[c].start()
        reg_copies[c].start()

    barrier = pltpu.get_barrier_semaphore()
    x_low, x_high = lax.rem(gx + groups_x - 1, groups_x), lax.rem(gx + 1, groups_x)
    y_low, y_high = lax.rem(gy + groups_y - 1, groups_y), lax.rem(gy + 1, groups_y)
    sides = ((x_low, gy), (x_high, gy), (gx, y_low), (gx, y_high))
    for i in range(1, groups_x):
        pl.semaphore_signal(
            barrier, inc=1, device_id=(lax.rem(gx + i, groups_x), gy), device_id_type=MESH
        )
    for i in range(1, groups_y):
        pl.semaphore_signal(
            barrier, inc=1, device_id=(gx, lax.rem(gy + i, groups_y)), device_id_type=MESH
        )

    vel_copy.wait()
    half_lanes = LANES // 2
    lanes8 = iota((ROWS, LANES), 1)
    row8 = iota((ROWS, LANES), 0)
    tiles = vel.shape[3] // LANES
    flow = [[vel[c, 0, :, m * LANES : (m + 1) * LANES] for m in range(tiles)] for c in range(3)]
    for m in range(tiles):
        turned = [pltpu.roll(flow[c][m], half_lanes, 1) for c in range(3)]
        for odd in range(2):
            first, second, third = (
                (turned[0], flow[1][m], turned[2]) if odd else (flow[0][m], turned[1], flow[2][m])
            )
            sv[2 * m + odd, 0] = jnp.where(lanes8 < half_lanes, first, second)
            tile = jnp.where(lanes8 < half_lanes, third, 0.0)
            for c in range(3):
                if odd:
                    below = flow[c][m][:, half_lanes - 1 : half_lanes]
                    above = flow[c][(m + 1) % tiles][:, 0:1]
                else:
                    below = flow[c][(m - 1) % tiles][:, LANES - 1 : LANES]
                    above = flow[c][m][:, half_lanes : half_lanes + 1]
                tile = jnp.where(lanes8 == half_lanes + c, below, tile)
                tile = jnp.where(lanes8 == half_lanes + 3 + c, above, tile)
            sv[2 * m + odd, 1] = tile
    s1[gx] = sv[gx]

    pl.semaphore_wait(barrier, groups_x + groups_y - 2)

    def send_x(i, _):
        t = lax.rem(gx + i, groups_x)
        pltpu.make_async_remote_copy(
            src_ref=sv.at[t], dst_ref=s1.at[gx], send_sem=vsend, recv_sem=vrecv,
            device_id=(t, gy), device_id_type=MESH,
        ).start()
        return 0

    lax.fori_loop(1, groups_x, send_x, 0)

    taps_copy.wait()
    owner_copy.wait()
    shape = (2 * LANES, cols)
    q, f = iota(shape, 0), iota(shape, 1)
    for c in range(3):
        place = q - c * half_lanes
        place = jnp.where((place >= 0) & (place < half_lanes), place, -100)
        place = jnp.where(q == 3 * half_lanes + c, -1, place)
        place = jnp.where(q == 3 * half_lanes + 3 + c, half_lanes, place)
        px[c, 0], px[c, 1] = split(tap_weights(taps, 0, f & 3, place - (f >> 2) + 1))
    shape = (rows, 12 * ROWS)
    f, q = iota(shape, 0), iota(shape, 1)
    third_part = q >= 8 * ROWS
    q = q & (4 * ROWS - 1)
    place = jnp.where(q < 2 * ROWS, q, -100)
    place = jnp.where((q == 2 * ROWS) | (q == 3 * ROWS + 2), -1, place)
    place = jnp.where((q == 2 * ROWS + 1) | (q == 3 * ROWS + 3), 2 * ROWS, place)
    weights = tap_weights(taps, 1, f & 3, place - (f >> 2) + 1) * (scale * 0.25)
    high = weights.astype(BF16).astype(F32)
    py[...] = jnp.where(third_part, weights - high, high).astype(BF16)
    high, low = split(difference((cols, cols), 0, 1))
    dx[0:cols, :] = high
    dx[cols : 2 * cols, :] = high
    dx[2 * cols : 3 * cols, :] = low
    high, low = split(difference((rows, rows), 1, 0))
    dy[...] = jnp.concatenate([high.astype(F32), high.astype(F32), low.astype(F32)], axis=1).astype(BF16)

    row_of = iota((rows, cols), 0)
    lane_of = iota((rows, cols), 1)
    edge_lane = iota((rows, LANES), 1)

    def base_of(c):
        reg_copies[c].wait()

        def base(z, _):
            b = nm[c, z]
            before = nm[c, lax.rem(z + depth - 1, depth)]
            after = nm[c, lax.rem(z + 1, depth)]
            total = before + after - 6.0 * b
            total = total + jnp.where(row_of == 0, 0.0, pltpu.roll(b, 1, 0))
            total = total + jnp.where(row_of == rows - 1, 0.0, pltpu.roll(b, rows - 1, 0))
            total = total + jnp.where(lane_of == 0, 0.0, pltpu.roll(b, 1, 1))
            total = total + jnp.where(lane_of == cols - 1, 0.0, pltpu.roll(b, cols - 1, 1))
            nr[c, z] = rk_keep * nr[c, z] + nu * total
            return 0

        steps(depth, UNROLL_BASE, base, 0)

    def exchange(xs, xr, ys, yr, ssem, rsem):
        copies = []
        for k in (2, 3, 0, 1):
            src, dst = (xs, xr) if k < 2 else (ys, yr)
            copies.append(
                pltpu.make_async_remote_copy(
                    src_ref=src.at[k % 2], dst_ref=dst.at[1 - k % 2],
                    send_sem=ssem.at[k], recv_sem=rsem.at[k],
                    device_id=sides[k], device_id_type=MESH,
                )
            )
            copies[-1].start()
        return copies

    edges = (jnp.zeros((rows, LANES), F32), jnp.zeros((rows, LANES), F32))
    for c in range(3):
        mag_copies[c].wait()

        def border(z, carry):
            low, high = carry
            bys[0, pl.ds(c * depth + z, 1), :] = nm[c, z, 0:1, :]
            bys[1, pl.ds(c * depth + z, 1), :] = nm[c, z, rows - 1 : rows, :]
            here = edge_lane == c * 32 + z
            low = jnp.where(here, nm[c, z, :, 0:1], low)
            high = jnp.where(here, nm[c, z, :, cols - 1 : cols], high)
            return low, high

        edges = steps(depth, UNROLL_BORDER, border, edges)
    bxs[0], bxs[1] = edges
    b_copies = exchange(bxs, bxr, bys, byr, bsend, brecv)

    base_of(0)

    others = s1.at[pl.ds(0, groups_x - 1)]
    pltpu.make_async_copy(others, others, vrecv).wait()
    for g in range(groups_y):
        below, above = (2 * g - 1) % groups_x, (2 * g + 2) % groups_x
        tile = jnp.zeros((ROWS, LANES), F32)
        for k in range(2):
            tile = jnp.where(row8 == 2 * k, s1[below, k, ROWS - 1 : ROWS, :], tile)
            tile = jnp.where(row8 == 2 * k + 1, s1[above, k, 0:1, :], tile)
        hs[g] = tile
    rv[gy] = s1[pl.ds(2 * gy, 2)]
    rh[gy] = hs[gy]

    def send_y(i, _):
        g = lax.rem(gy + i, groups_y)
        pltpu.make_async_remote_copy(
            src_ref=s1.at[pl.ds(2 * g, 2)], dst_ref=rv.at[gy], send_sem=wsend, recv_sem=wrecv,
            device_id=(gx, g), device_id_type=MESH,
        ).start()
        pltpu.make_async_remote_copy(
            src_ref=hs.at[g], dst_ref=rh.at[gy], send_sem=hsend, recv_sem=hrecv,
            device_id=(gx, g), device_id_type=MESH,
        ).start()
        return 0

    lax.fori_loop(1, groups_y, send_y, 0)

    base_of(1)
    base_of(2)

    for copy in b_copies:
        copy.wait_recv()
    first_row = jnp.where(iota((ROWS, cols), 0) == 0, nu, 0.0)
    last_row = jnp.where(iota((ROWS, cols), 0) == ROWS - 1, nu, 0.0)
    first_lane = jnp.where(iota((1, LANES), 1) == 0, nu, 0.0)
    last_lane = jnp.where(iota((1, LANES), 1) == LANES - 1, nu, 0.0)

    def beside_cells(i, _):
        back = lax.rem(LANES - i * UNROLL_BESIDE, LANES)
        near = [pltpu.roll(bxr[k], back, 1) for k in range(2)]
        for k in range(UNROLL_BESIDE):
            z = i * UNROLL_BESIDE + k
            for c in range(3):
                at = c * 32 + k
                lo = near[0][:, at : at + 1] * first_lane
                hi = near[1][:, at : at + 1] * last_lane
                total = nr[c, z] + jnp.concatenate([lo, hi], axis=1)
                top = byr[0, pl.ds(c * depth + z, 1), :] * first_row
                bottom = byr[1, pl.ds(c * depth + z, 1), :] * last_row
                nr[c, z] = jnp.concatenate(
                    [total[:ROWS] + top, total[ROWS : rows - ROWS], total[rows - ROWS :] + bottom], axis=0
                )
        return 0

    lax.fori_loop(0, depth // UNROLL_BESIDE, beside_cells, 0)

    others = rv.at[pl.ds(0, planes - 1)]
    pltpu.make_async_copy(others, others, wrecv).wait()
    others = rh.at[pl.ds(0, planes - 1)]
    pltpu.make_async_copy(others, others, hrecv).wait()
    main = 2 * ROWS * planes
    blocks = [rv[:, :, k].reshape(main, LANES) for k in range(2)]
    beside = rh[...].reshape(ROWS * planes, LANES)
    blank = jnp.zeros_like(beside)
    coarse = jnp.concatenate(
        [
            jnp.concatenate(blocks, axis=1),
            jnp.concatenate([beside, blank], axis=1),
            jnp.concatenate([blank, beside], axis=1),
        ],
        axis=0,
    )
    high, low = split(coarse)
    for c in range(3):
        xc[c] = dot(high, px[c, 0]) + dot(low, px[c, 0]) + dot(high, px[c, 1])
    for p in range(planes):
        for c in range(3):
            a0 = main + p * ROWS
            b0 = a0 + planes * ROWS
            near = jnp.concatenate(
                [
                    xc[c, p * 2 * ROWS : (p + 1) * 2 * ROWS, :],
                    xc[c, a0 : a0 + ROWS, :],
                    xc[c, b0 : b0 + ROWS, :],
                ],
                axis=0,
            )
            high, low = split(near)
            u[c, p] = dot(py[...], jnp.concatenate([high, low, high], axis=0))

    strip = 2 * ROWS
    lane_low = powers((1, LANES), 1, False)
    lane_high = powers((1, LANES), 1, True)
    sub_low = powers((strip, cols), 0, False)
    sub_high = powers((strip, cols), 0, True)
    strip_lane = iota((strip, LANES), 1)
    weights_z = [[taps[2, o, s] for s in range(3)] for o in range(R)]

    def stored(p):
        at = jnp.int32(0)
        for b in range(planes):
            at = jnp.where(owner[b] == p, b, at)
        return at

    def strips(j, _):
        r0 = pl.multiple_of(j * strip, strip)

        def cross(p, carry):
            low, high = carry
            around = [stored(lax.rem(p + planes + s - 1, planes)) for s in range(3)]
            for o in range(R):
                z = p * R + o
                us = []
                for c in range(3):
                    total = weights_z[o][0] * u[c, around[0], pl.ds(r0, strip), :]
                    total = total + weights_z[o][1] * u[c, around[1], pl.ds(r0, strip), :]
                    us.append(total + weights_z[o][2] * u[c, around[2], pl.ds(r0, strip), :])
                bs = [nm[c, z, pl.ds(r0, strip), :] for c in range(3)]
                for c in range(3):
                    a, b = (c + 1) % 3, (c + 2) % 3
                    e = us[a] * bs[b] - us[b] * bs[a]
                    ub[c, z, pl.ds(r0, strip), :] = e
                    if c > 0:
                        here = strip_lane == (c - 1) * 32 + z
                        sum_low = jnp.sum(e[:, :LANES] * lane_low, axis=1, keepdims=True)
                        sum_high = jnp.sum(e[:, cols - LANES :] * lane_high, axis=1, keepdims=True)
                        low = jnp.where(here, sum_low, low)
                        high = jnp.where(here, sum_high, high)
            return low, high

        zeros = jnp.zeros((strip, LANES), F32)
        low, high = steps(planes, UNROLL_CROSS, cross, (zeros, zeros))
        exs[0, pl.ds(r0, strip), :] = low
        exs[1, pl.ds(r0, strip), :] = high
        return 0

    lax.fori_loop(0, rows // strip, strips, 0)

    def edge(z, _):
        for k, c in enumerate((0, 2)):
            at = pl.ds(k * depth + z, 1)
            eys[0, at, :] = jnp.sum(ub[c, z, 0:strip, :] * sub_low, axis=0, keepdims=True)
            eys[1, at, :] = jnp.sum(ub[c, z, rows - strip : rows, :] * sub_high, axis=0, keepdims=True)
        return 0

    steps(depth, UNROLL_EDGE, edge, 0)
    e_copies = exchange(exs, exr, eys, eyr, esend, erecv)

    warm = TAIL if depth > TAIL else depth
    wrap = 1.0 if depth > TAIL else 1.0 / (1.0 - decay**depth)

    def strips_z(j, _):
        r0 = pl.multiple_of(j * strip, strip)
        part = pl.ds(r0, strip)

        def warm_up(i, carry):
            bx, by, ax, ay = carry
            z = depth - warm + i
            bx = ub[0, z, part, :] + decay * bx
            by = ub[1, z, part, :] + decay * by
            z = warm - 1 - i
            ax = ub[0, z, part, :] + decay * ax
            ay = ub[1, z, part, :] + decay * ay
            return bx, by, ax, ay

        zeros = jnp.zeros((strip, cols), F32)
        carry = steps(warm, UNROLL_Z, warm_up, (zeros,) * 4)
        if wrap != 1.0:
            carry = tuple(wrap * value for value in carry)

        def along_z(i, carry):
            bx, by, ax, ay = carry
            z = i
            nr[1, z, part, :] += -bx
            nr[0, z, part, :] += by
            bx = ub[0, z, part, :] + decay * bx
            by = ub[1, z, part, :] + decay * by
            z = depth - 1 - i
            nr[1, z, part, :] += ax
            nr[0, z, part, :] += -ay
            ax = ub[0, z, part, :] + decay * ax
            ay = ub[1, z, part, :] + decay * ay
            return bx, by, ax, ay

        steps(depth, UNROLL_Z, along_z, carry)
        return 0

    lax.fori_loop(0, rows // strip, strips_z, 0)

    def group(i, _):
        at = pl.ds(i * GROUP, GROUP)
        parts = []
        for c in range(3):
            high, low = split(ub[c, at].reshape(GROUP * rows, cols))
            parts.append((high, low))
        along_x = [
            dot(jnp.concatenate([high, low, high], axis=1), dx[...]).reshape(GROUP, rows, cols)
            for high, low in (parts[1], parts[2])
        ]
        nr[1, at] += -along_x[1]
        for k in range(GROUP):
            z = i * GROUP + k
            cut = slice(k * rows, (k + 1) * rows)
            along_y = [
                dot(dy[...], jnp.concatenate([high[cut], low[cut], high[cut]], axis=0))
                for high, low in (parts[0], parts[2])
            ]
            nr[0, z] += along_y[1]
            nr[2, z] += along_x[0][k] - along_y[0]
        return 0

    lax.fori_loop(0, depth // GROUP, group, 0)

    for copy in e_copies:
        copy.wait_recv()
    for copy in b_copies + e_copies:
        copy.wait_send()
    for ref, sem, count in ((sv, vsend, groups_x), (rv, wsend, groups_y), (rh, hsend, groups_y)):
        part = ref.at[pl.ds(0, count - 1)]
        pltpu.make_async_copy(part, part, sem).wait()


def update_kernel(b, partial, exr, eyr, mag_hbm, reg_hbm, nm, nr, sems):
    _, depth, rows, cols = b.shape
    strip = 2 * ROWS
    lane_low = powers((1, LANES), 1, False)
    lane_high = powers((1, LANES), 1, True)
    sub_low = powers((strip, cols), 0, False)
    sub_high = powers((strip, cols), 0, True)

    def planes(i, _):
        back = lax.rem(LANES - i * OUT, LANES)
        near = [pltpu.roll(exr[k], back, 1) for k in range(2)]
        for k in range(OUT):
            z = i * OUT + k
            for c in range(3):
                total = partial[c, z]
                if c == 1:
                    lo = near[0][:, 32 + k : 33 + k] * lane_low
                    hi = near[1][:, 32 + k : 33 + k] * lane_high
                    total = total + jnp.concatenate([lo, -hi], axis=1)
                if c == 2:
                    lo = near[0][:, k : k + 1] * lane_low
                    hi = near[1][:, k : k + 1] * lane_high
                    total = total - jnp.concatenate([lo, -hi], axis=1)
                if c != 1:
                    at = pl.ds(z if c == 2 else depth + z, 1)
                    top = eyr[0, at, :] * sub_low
                    bottom = eyr[1, at, :] * sub_high
                    first, last = total[:strip], total[rows - strip :]
                    first, last = (first - top, last + bottom) if c == 0 else (first + top, last - bottom)
                    total = jnp.concatenate([first, total[strip : rows - strip], last], axis=0)
                nr[c, z] = total
                nm[c, z] = b[c, z] + rk_gain * total
        at = pl.ds(i * OUT, OUT)
        for c in range(3):
            pltpu.make_async_copy(nr.at[c, at], reg_hbm.at[c, at], sems.at[0]).start()
            pltpu.make_async_copy(nm.at[c, at], mag_hbm.at[c, at], sems.at[1]).start()
        return 0

    lax.fori_loop(0, depth // OUT, planes, 0)
    pltpu.make_async_copy(nr, reg_hbm, sems.at[0]).wait()
    pltpu.make_async_copy(nm, mag_hbm, sems.at[1]).wait()


def body(groups_x, groups_y, magnetic, register, velocity, prolong_taps, owner_map):
    shape = magnetic.shape
    _, depth, rows, cols = shape
    planes = groups_y
    spacing = 2.0 * math.pi / (cols * groups_x)
    nu = 2.0 * math.pi / reynolds / (4.0 * spacing)
    brick = pltpu.VMEM(shape, F32)
    dma = pltpu.SemaphoreType.DMA
    args = [
        pltpu.with_memory_space_constraint(x, pltpu.HBM)
        for x in (prolong_taps, owner_map, magnetic, register, velocity)
    ]
    made = pl.pallas_call(
        functools.partial(kernel, groups_x, groups_y, nu),
        out_shape=(
            brick, brick, pltpu.VMEM((2, rows, LANES), F32), pltpu.VMEM((2, 2 * depth, cols), F32)
        ),
        in_specs=[pl.BlockSpec(memory_space=pltpu.HBM)] * 5,
        out_specs=(pl.BlockSpec(memory_space=pltpu.VMEM),) * 4,
        scratch_shapes=[
            pltpu.SMEM(prolong_taps.shape, F32),
            pltpu.SMEM(owner_map.shape, jnp.int32),
            pltpu.VMEM(velocity.shape, F32),
            pltpu.VMEM((groups_x, 2, ROWS, LANES), F32),
            pltpu.VMEM((groups_x, 2, ROWS, LANES), F32),
            pltpu.VMEM((groups_y, ROWS, LANES), F32),
            pltpu.VMEM((planes, 2, 2, ROWS, LANES), F32),
            pltpu.VMEM((planes, ROWS, LANES), F32),
            pltpu.VMEM((2, rows, LANES), F32),
            pltpu.VMEM((2, rows, LANES), F32),
            pltpu.VMEM((2, 3 * depth, cols), F32),
            pltpu.VMEM((2, 3 * depth, cols), F32),
            pltpu.VMEM((2, rows, LANES), F32),
            pltpu.VMEM((2, 2 * depth, cols), F32),
            pltpu.VMEM((3, 2, 2 * LANES, cols), BF16),
            pltpu.VMEM((rows, 12 * ROWS), BF16),
            pltpu.VMEM((3, 4 * ROWS * planes, cols), F32),
            pltpu.VMEM((3, planes, rows, cols), F32),
            pltpu.VMEM(shape, F32),
            pltpu.VMEM((3 * cols, cols), BF16),
            pltpu.VMEM((rows, 3 * rows), BF16),
            dma((6,)), dma((3,)), dma, dma, dma, dma, dma, dma,
            dma((4,)), dma((4,)), dma((4,)), dma((4,)),
        ],
        compiler_params=pltpu.CompilerParams(
            collective_id=0, has_side_effects=True, vmem_limit_bytes=40 << 20
        ),
    )(*args)
    made = [pltpu.with_memory_space_constraint(x, pltpu.VMEM) for x in made]
    out = jax.ShapeDtypeStruct(shape, F32)
    return pl.pallas_call(
        update_kernel,
        out_shape=(out, out),
        in_specs=[pl.BlockSpec(memory_space=pltpu.VMEM)] * 4,
        out_specs=(pl.BlockSpec(memory_space=pltpu.HBM),) * 2,
        scratch_shapes=[pltpu.VMEM(shape, F32), pltpu.VMEM(shape, F32), dma((2,))],
        compiler_params=pltpu.CompilerParams(vmem_limit_bytes=20 << 20),
    )(*made)


def solution(mesh):
    brick = P(None, None, "gy", "gx")
    return jax.shard_map(
        functools.partial(body, mesh.shape["gx"], mesh.shape["gy"]),
        mesh=mesh,
        in_specs=(brick, brick, P(None, "gy", "gx", None), P(), P()),
        out_specs=(brick, brick),
        check_vma=False,
    )
```

```python
import functools
import math

import jax
import jax.numpy as jnp
from jax import lax
from jax.experimental import pallas as pl
from jax.experimental.pallas import tpu as pltpu
from jax.sharding import PartitionSpec as P

MESH = pl.DeviceIdType.MESH
F32 = jnp.float32
BF16 = jnp.bfloat16

R = 4
LANES = 128
ROWS = 8
UNROLL_BORDER = 8
UNROLL_BASE = 4
UNROLL_CROSS = 2
UNROLL_EDGE = 8
UNROLL_Z = 8
GROUP = 8
OUT = 4
TAIL = 16

alpha_pade = 0.25
coef_pade = 1.5
rk_keep = -5.0 / 9.0
rk_gain = 15.0 / 16.0
reynolds = 10000.0
decay = (-1.0 + math.sqrt(1.0 - 4.0 * alpha_pade * alpha_pade)) / (2.0 * alpha_pade)
scale = coef_pade / 2.0 * (1.0 + decay * decay)


def split(value):
    high = value.astype(BF16)
    low = (value - high.astype(F32)).astype(BF16)
    return high, low


def iota(shape, dim):
    return lax.broadcasted_iota(jnp.int32, shape, dim)


def tap_weights(taps, axis, offset, neighbour):
    out = jnp.zeros(offset.shape, F32)
    for o in range(R):
        for s in range(3):
            out = jnp.where((offset == o) & (neighbour == s), taps[axis, o, s], out)
    return out


def powers(shape, dim, flip):
    index = iota(shape, dim)
    if flip:
        index = shape[dim] - 1 - index
    magnitude = jnp.exp(index.astype(F32) * math.log(abs(decay)))
    return jnp.where((index & 1) == 1, -magnitude, magnitude)


def steps(count, unroll, body, carry):
    def outer(i, carry):
        for k in range(unroll):
            carry = body(i * unroll + k, carry)
        return carry

    return lax.fori_loop(0, count // unroll, outer, carry)


def difference(shape, dim_source, dim_target):
    step = iota(shape, dim_source) - iota(shape, dim_target)
    size = jnp.maximum(jnp.abs(step) - 1, 0)
    magnitude = jnp.exp(size.astype(F32) * math.log(abs(decay)))
    signed = jnp.where((size & 1) == 1, -magnitude, magnitude)
    return jnp.where(step > 0, signed, jnp.where(step < 0, -signed, 0.0))


def dot(a, b):
    return jnp.dot(a, b, preferred_element_type=F32)


def kernel(
    groups_x, groups_y, nu,
    taps_hbm, owner_hbm, mag_hbm, reg_hbm, vel_hbm,
    nm, nr, exr, eyr, ub, dy,
    taps, owner, vel, sv, s1, hs, rv, rh, bxs, bxr, bys, byr, exs, eys,
    px, py, xc, u, dx,
    in_sem, const_sem, vsend, vrecv, wsend, wrecv, hsend, hrecv, bsend, brecv, esend, erecv,
):
    gx, gy = lax.axis_index("gx"), lax.axis_index("gy")
    _, depth, rows, cols = nm.shape
    planes = groups_y

    vel_copy = pltpu.make_async_copy(vel_hbm, vel, const_sem.at[0])
    vel_copy.start()
    taps_copy = pltpu.make_async_copy(taps_hbm, taps, const_sem.at[1])
    owner_copy = pltpu.make_async_copy(owner_hbm, owner, const_sem.at[2])
    taps_copy.start()
    owner_copy.start()
    mag_copies, reg_copies = [], []
    for c in range(3):
        mag_copies.append(pltpu.make_async_copy(mag_hbm.at[c], nm.at[c], in_sem.at[c]))
        reg_copies.append(pltpu.make_async_copy(reg_hbm.at[c], nr.at[c], in_sem.at[3 + c]))
        mag_copies[c].start()
        reg_copies[c].start()

    barrier = pltpu.get_barrier_semaphore()
    x_low, x_high = lax.rem(gx + groups_x - 1, groups_x), lax.rem(gx + 1, groups_x)
    y_low, y_high = lax.rem(gy + groups_y - 1, groups_y), lax.rem(gy + 1, groups_y)
    sides = ((x_low, gy), (x_high, gy), (gx, y_low), (gx, y_high))
    far_x = sorted(range(1, groups_x), key=lambda i: abs(i - groups_x // 2))
    far_y = sorted(range(1, groups_y), key=lambda i: abs(i - groups_y // 2))
    for i in far_x:
        pl.semaphore_signal(
            barrier, inc=1, device_id=(lax.rem(gx + i, groups_x), gy), device_id_type=MESH
        )
    for i in far_y:
        pl.semaphore_signal(
            barrier, inc=1, device_id=(gx, lax.rem(gy + i, groups_y)), device_id_type=MESH
        )

    vel_copy.wait()
    half_lanes = LANES // 2
    lanes8 = iota((ROWS, LANES), 1)
    row8 = iota((ROWS, LANES), 0)
    tiles = vel.shape[3] // LANES
    flow = [[vel[c, 0, :, m * LANES : (m + 1) * LANES] for m in range(tiles)] for c in range(3)]
    for m in range(tiles):
        turned = [pltpu.roll(flow[c][m], half_lanes, 1) for c in range(3)]
        for odd in range(2):
            first, second, third = (
                (turned[0], flow[1][m], turned[2]) if odd else (flow[0][m], turned[1], flow[2][m])
            )
            sv[2 * m + odd, 0] = jnp.where(lanes8 < half_lanes, first, second)
            tile = jnp.where(lanes8 < half_lanes, third, 0.0)
            for c in range(3):
                if odd:
                    below = flow[c][m][:, half_lanes - 1 : half_lanes]
                    above = flow[c][(m + 1) % tiles][:, 0:1]
                else:
                    below = flow[c][(m - 1) % tiles][:, LANES - 1 : LANES]
                    above = flow[c][m][:, half_lanes : half_lanes + 1]
                tile = jnp.where(lanes8 == half_lanes + c, below, tile)
                tile = jnp.where(lanes8 == half_lanes + 3 + c, above, tile)
            sv[2 * m + odd, 1] = tile
    s1[gx] = sv[gx]

    pl.semaphore_wait(barrier, groups_x + groups_y - 2)

    for i in far_x:
        t = lax.rem(gx + i, groups_x)
        pltpu.make_async_remote_copy(
            src_ref=sv.at[t], dst_ref=s1.at[gx], send_sem=vsend, recv_sem=vrecv,
            device_id=(t, gy), device_id_type=MESH,
        ).start()

    taps_copy.wait()
    owner_copy.wait()
    shape = (2 * LANES, cols)
    q, f = iota(shape, 0), iota(shape, 1)
    for c in range(3):
        place = q - c * half_lanes
        place = jnp.where((place >= 0) & (place < half_lanes), place, -100)
        place = jnp.where(q == 3 * half_lanes + c, -1, place)
        place = jnp.where(q == 3 * half_lanes + 3 + c, half_lanes, place)
        px[c, 0], px[c, 1] = split(tap_weights(taps, 0, f & 3, place - (f >> 2) + 1))
    shape = (rows, 12 * ROWS)
    f, q = iota(shape, 0), iota(shape, 1)
    third_part = q >= 8 * ROWS
    q = q & (4 * ROWS - 1)
    place = jnp.where(q < 2 * ROWS, q, -100)
    place = jnp.where((q == 2 * ROWS) | (q == 3 * ROWS + 2), -1, place)
    place = jnp.where((q == 2 * ROWS + 1) | (q == 3 * ROWS + 3), 2 * ROWS, place)
    weights = tap_weights(taps, 1, f & 3, place - (f >> 2) + 1) * (scale * 0.25)
    high = weights.astype(BF16).astype(F32)
    py[...] = jnp.where(third_part, weights - high, high).astype(BF16)
    high, low = split(difference((cols, cols), 0, 1))
    dx[0:cols, :] = high
    dx[cols : 2 * cols, :] = high
    dx[2 * cols : 3 * cols, :] = low
    high, low = split(difference((rows, rows), 1, 0))
    dy[...] = jnp.concatenate([high.astype(F32), high.astype(F32), low.astype(F32)], axis=1).astype(BF16)

    row_of = iota((rows, cols), 0)
    lane_of = iota((rows, cols), 1)
    edge_lane = iota((rows, LANES), 1)

    def base_of(c):
        reg_copies[c].wait()

        def base(z, _):
            b = nm[c, z]
            before = nm[c, lax.rem(z + depth - 1, depth)]
            after = nm[c, lax.rem(z + 1, depth)]
            total = before + after - 6.0 * b
            total = total + jnp.where(row_of == 0, 0.0, pltpu.roll(b, 1, 0))
            total = total + jnp.where(row_of == rows - 1, 0.0, pltpu.roll(b, rows - 1, 0))
            total = total + jnp.where(lane_of == 0, 0.0, pltpu.roll(b, 1, 1))
            total = total + jnp.where(lane_of == cols - 1, 0.0, pltpu.roll(b, cols - 1, 1))
            nr[c, z] = rk_keep * nr[c, z] + nu * total
            return 0

        steps(depth, UNROLL_BASE, base, 0)

    def exchange(xs, xr, ys, yr, ssem, rsem, which=(2, 3, 0, 1)):
        copies = []
        for k in which:
            src, dst = (xs, xr) if k < 2 else (ys, yr)
            copies.append(
                pltpu.make_async_remote_copy(
                    src_ref=src.at[k % 2], dst_ref=dst.at[1 - k % 2],
                    send_sem=ssem.at[k], recv_sem=rsem.at[k],
                    device_id=sides[k], device_id_type=MESH,
                )
            )
            copies[-1].start()
        return copies

    edges = (jnp.zeros((rows, LANES), F32), jnp.zeros((rows, LANES), F32))
    for c in range(3):
        mag_copies[c].wait()

        def border(z, carry):
            low, high = carry
            bys[0, pl.ds(c * depth + z, 1), :] = nm[c, z, 0:1, :]
            bys[1, pl.ds(c * depth + z, 1), :] = nm[c, z, rows - 1 : rows, :]
            here = edge_lane == c * 32 + z
            low = jnp.where(here, nm[c, z, :, 0:1], low)
            high = jnp.where(here, nm[c, z, :, cols - 1 : cols], high)
            return low, high

        edges = steps(depth, UNROLL_BORDER, border, edges)
    bxs[0], bxs[1] = edges

    base_of(0)

    others = s1.at[pl.ds(0, groups_x - 1)]
    pltpu.make_async_copy(others, others, vrecv).wait()
    for g in range(groups_y):
        below, above = (2 * g - 1) % groups_x, (2 * g + 2) % groups_x
        tile = jnp.zeros((ROWS, LANES), F32)
        for k in range(2):
            tile = jnp.where(row8 == 2 * k, s1[below, k, ROWS - 1 : ROWS, :], tile)
            tile = jnp.where(row8 == 2 * k + 1, s1[above, k, 0:1, :], tile)
        hs[g] = tile
    rv[gy] = s1[pl.ds(2 * gy, 2)]
    rh[gy] = hs[gy]

    for i in far_y:
        g = lax.rem(gy + i, groups_y)
        pltpu.make_async_remote_copy(
            src_ref=s1.at[pl.ds(2 * g, 2)], dst_ref=rv.at[gy], send_sem=wsend, recv_sem=wrecv,
            device_id=(gx, g), device_id_type=MESH,
        ).start()
        pltpu.make_async_remote_copy(
            src_ref=hs.at[g], dst_ref=rh.at[gy], send_sem=hsend, recv_sem=hrecv,
            device_id=(gx, g), device_id_type=MESH,
        ).start()

    b_copies = exchange(bxs, bxr, bys, byr, bsend, brecv)
    base_of(1)
    base_of(2)

    others = rv.at[pl.ds(0, planes - 1)]
    pltpu.make_async_copy(others, others, wrecv).wait()
    others = rh.at[pl.ds(0, planes - 1)]
    pltpu.make_async_copy(others, others, hrecv).wait()
    main = 2 * ROWS * planes
    blocks = [rv[:, :, k].reshape(main, LANES) for k in range(2)]
    beside = rh[...].reshape(ROWS * planes, LANES)
    blank = jnp.zeros_like(beside)
    coarse = jnp.concatenate(
        [
            jnp.concatenate(blocks, axis=1),
            jnp.concatenate([beside, blank], axis=1),
            jnp.concatenate([blank, beside], axis=1),
        ],
        axis=0,
    )
    high, low = split(coarse)
    for c in range(3):
        xc[c] = dot(high, px[c, 0]) + dot(low, px[c, 0]) + dot(high, px[c, 1])
    for p in range(planes):
        for c in range(3):
            a0 = main + p * ROWS
            b0 = a0 + planes * ROWS
            near = jnp.concatenate(
                [
                    xc[c, p * 2 * ROWS : (p + 1) * 2 * ROWS, :],
                    xc[c, a0 : a0 + ROWS, :],
                    xc[c, b0 : b0 + ROWS, :],
                ],
                axis=0,
            )
            high, low = split(near)
            u[c, p] = dot(py[...], jnp.concatenate([high, low, high], axis=0))

    strip = 2 * ROWS
    lane_low = powers((1, LANES), 1, False)
    lane_high = powers((1, LANES), 1, True)
    sub_low = powers((strip, cols), 0, False)
    sub_high = powers((strip, cols), 0, True)
    weights_z = [[taps[2, o, n] for n in range(3)] for o in range(R)]

    def stored(p):
        at = jnp.int32(0)
        for b in range(planes):
            at = jnp.where(owner[b] == p, b, at)
        return at

    def strips(j, _):
        part = pl.ds(pl.multiple_of(j * ROWS, ROWS), ROWS)

        def cross(p, carry):
            low, high = carry
            around = [stored(lax.rem(p + planes + n - 1, planes)) for n in range(3)]
            near = [[u[c, around[n], part, :] for n in range(3)] for c in range(3)]
            for o in range(R):
                z = p * R + o
                us = []
                for c in range(3):
                    total = weights_z[o][0] * near[c][0] + weights_z[o][1] * near[c][1]
                    us.append(total + weights_z[o][2] * near[c][2])
                bs = [nm[c, z, part, :] for c in range(3)]
                for c in range(3):
                    a, b = (c + 1) % 3, (c + 2) % 3
                    e = us[a] * bs[b] - us[b] * bs[a]
                    ub[c, z, part, :] = e
                    if c > 0:
                        here = lanes8 == (c - 1) * 32 + z
                        sum_low = jnp.sum(e[:, :LANES] * lane_low, axis=1, keepdims=True)
                        sum_high = jnp.sum(e[:, cols - LANES :] * lane_high, axis=1, keepdims=True)
                        low = jnp.where(here, sum_low, low)
                        high = jnp.where(here, sum_high, high)
            return low, high

        zeros = jnp.zeros((ROWS, LANES), F32)
        low, high = steps(planes, UNROLL_CROSS, cross, (zeros, zeros))
        exs[0, part, :] = low
        exs[1, part, :] = high
        return 0

    count = rows // ROWS
    lax.fori_loop(0, 4, lambda k, _: strips(k + (count - 4) * (k // 2), 0), 0)

    def edge(z, _):
        for k, c in enumerate((0, 2)):
            at = pl.ds(k * depth + z, 1)
            eys[0, at, :] = jnp.sum(ub[c, z, 0:strip, :] * sub_low, axis=0, keepdims=True)
            eys[1, at, :] = jnp.sum(ub[c, z, rows - strip : rows, :] * sub_high, axis=0, keepdims=True)
        return 0

    steps(depth, UNROLL_EDGE, edge, 0)
    e_copies = exchange(exs, exr, eys, eyr, esend, erecv, (2, 3))
    lax.fori_loop(2, count - 2, strips, 0)
    e_copies = e_copies + exchange(exs, exr, eys, eyr, esend, erecv, (0, 1))

    warm = TAIL if depth > TAIL else depth
    wrap = 1.0 if depth > TAIL else 1.0 / (1.0 - decay**depth)

    def strips_z(j, _):
        r0 = pl.multiple_of(j * strip, strip)
        part = pl.ds(r0, strip)

        def warm_up(i, carry):
            bx, by, ax, ay = carry
            z = depth - warm + i
            bx = ub[0, z, part, :] + decay * bx
            by = ub[1, z, part, :] + decay * by
            z = warm - 1 - i
            ax = ub[0, z, part, :] + decay * ax
            ay = ub[1, z, part, :] + decay * ay
            return bx, by, ax, ay

        zeros = jnp.zeros((strip, cols), F32)
        carry = steps(warm, UNROLL_Z, warm_up, (zeros,) * 4)
        if wrap != 1.0:
            carry = tuple(wrap * value for value in carry)

        def along_z(i, carry):
            bx, by, ax, ay = carry
            z = i
            nr[1, z, part, :] += -bx
            nr[0, z, part, :] += by
            bx = ub[0, z, part, :] + decay * bx
            by = ub[1, z, part, :] + decay * by
            z = depth - 1 - i
            nr[1, z, part, :] += ax
            nr[0, z, part, :] += -ay
            ax = ub[0, z, part, :] + decay * ax
            ay = ub[1, z, part, :] + decay * ay
            return bx, by, ax, ay

        steps(depth, UNROLL_Z, along_z, carry)
        return 0

    lax.fori_loop(0, rows // strip, strips_z, 0)

    first_row = jnp.where(iota((ROWS, cols), 0) == 0, nu, 0.0)
    last_row = jnp.where(iota((ROWS, cols), 0) == ROWS - 1, nu, 0.0)
    first_lane = jnp.where(iota((1, LANES), 1) == 0, nu, 0.0)
    last_lane = jnp.where(iota((1, LANES), 1) == LANES - 1, nu, 0.0)
    for copy in b_copies:
        copy.wait_recv()

    def group(i, _):
        at = pl.ds(i * GROUP, GROUP)
        back = lax.rem(LANES - i * GROUP, LANES)
        near = [pltpu.roll(bxr[k], back, 1) for k in range(2)]
        along_x = []
        for c in (1, 2):
            high, low = split(ub[c, at].reshape(GROUP * rows, cols))
            out = dot(jnp.concatenate([high, low, high], axis=1), dx[...])
            along_x.append(out.reshape(GROUP, rows, cols))
        for k in range(GROUP):
            z = i * GROUP + k
            for c in range(3):
                spot = c * 32 + k
                lo = near[0][:, spot : spot + 1] * first_lane
                hi = near[1][:, spot : spot + 1] * last_lane
                total = nr[c, z] + jnp.concatenate([lo, hi], axis=1)
                if c == 1:
                    total = total - along_x[1][k]
                if c == 2:
                    total = total + along_x[0][k]
                top = byr[0, pl.ds(c * depth + z, 1), :] * first_row
                bottom = byr[1, pl.ds(c * depth + z, 1), :] * last_row
                nr[c, z] = jnp.concatenate(
                    [total[:ROWS] + top, total[ROWS : rows - ROWS], total[rows - ROWS :] + bottom], axis=0
                )
        return 0

    lax.fori_loop(0, depth // GROUP, group, 0)

    for copy in e_copies:
        copy.wait_recv()
    for copy in b_copies + e_copies:
        copy.wait_send()
    for ref, sem, count in ((sv, vsend, groups_x), (rv, wsend, groups_y), (rh, hsend, groups_y)):
        part = ref.at[pl.ds(0, count - 1)]
        pltpu.make_async_copy(part, part, sem).wait()


def update_kernel(b, partial, exr, eyr, ub, dy, mag_hbm, reg_hbm, nm, nr, sems):
    _, depth, rows, cols = b.shape
    strip = 2 * ROWS
    lane_low = powers((1, LANES), 1, False)
    lane_high = powers((1, LANES), 1, True)
    sub_low = powers((strip, cols), 0, False)
    sub_high = powers((strip, cols), 0, True)

    def planes(i, _):
        back = lax.rem(LANES - i * OUT, LANES)
        near = [pltpu.roll(exr[k], back, 1) for k in range(2)]
        for k in range(OUT):
            z = i * OUT + k
            for c in range(3):
                total = partial[c, z]
                if c != 1:
                    high, low = split(ub[2 - c, z])
                    out = dot(dy[...], jnp.concatenate([high, low, high], axis=0))
                    total = total + out if c == 0 else total - out
                if c == 1:
                    lo = near[0][:, 32 + k : 33 + k] * lane_low
                    hi = near[1][:, 32 + k : 33 + k] * lane_high
                    total = total + jnp.concatenate([lo, -hi], axis=1)
                if c == 2:
                    lo = near[0][:, k : k + 1] * lane_low
                    hi = near[1][:, k : k + 1] * lane_high
                    total = total - jnp.concatenate([lo, -hi], axis=1)
                if c != 1:
                    at = pl.ds(z if c == 2 else depth + z, 1)
                    top = eyr[0, at, :] * sub_low
                    bottom = eyr[1, at, :] * sub_high
                    first, last = total[:strip], total[rows - strip :]
                    first, last = (first - top, last + bottom) if c == 0 else (first + top, last - bottom)
                    total = jnp.concatenate([first, total[strip : rows - strip], last], axis=0)
                nr[c, z] = total
                nm[c, z] = b[c, z] + rk_gain * total
        at = pl.ds(i * OUT, OUT)
        for c in range(3):
            pltpu.make_async_copy(nr.at[c, at], reg_hbm.at[c, at], sems.at[0]).start()
            pltpu.make_async_copy(nm.at[c, at], mag_hbm.at[c, at], sems.at[1]).start()
        return 0

    lax.fori_loop(0, depth // OUT, planes, 0)
    pltpu.make_async_copy(nr, reg_hbm, sems.at[0]).wait()
    pltpu.make_async_copy(nm, mag_hbm, sems.at[1]).wait()


def body(groups_x, groups_y, magnetic, register, velocity, prolong_taps, owner_map):
    shape = magnetic.shape
    _, depth, rows, cols = shape
    planes = groups_y
    spacing = 2.0 * math.pi / (cols * groups_x)
    nu = 2.0 * math.pi / reynolds / (4.0 * spacing)
    brick = pltpu.VMEM(shape, F32)
    dma = pltpu.SemaphoreType.DMA
    args = [
        pltpu.with_memory_space_constraint(x, pltpu.HBM)
        for x in (prolong_taps, owner_map, magnetic, register, velocity)
    ]
    made = pl.pallas_call(
        functools.partial(kernel, groups_x, groups_y, nu),
        out_shape=(
            brick, brick, pltpu.VMEM((2, rows, LANES), F32), pltpu.VMEM((2, 2 * depth, cols), F32),
            brick, pltpu.VMEM((rows, 3 * rows), BF16),
        ),
        in_specs=[pl.BlockSpec(memory_space=pltpu.HBM)] * 5,
        out_specs=(pl.BlockSpec(memory_space=pltpu.VMEM),) * 6,
        scratch_shapes=[
            pltpu.SMEM(prolong_taps.shape, F32),
            pltpu.SMEM(owner_map.shape, jnp.int32),
            pltpu.VMEM(velocity.shape, F32),
            pltpu.VMEM((groups_x, 2, ROWS, LANES), F32),
            pltpu.VMEM((groups_x, 2, ROWS, LANES), F32),
            pltpu.VMEM((groups_y, ROWS, LANES), F32),
            pltpu.VMEM((planes, 2, 2, ROWS, LANES), F32),
            pltpu.VMEM((planes, ROWS, LANES), F32),
            pltpu.VMEM((2, rows, LANES), F32),
            pltpu.VMEM((2, rows, LANES), F32),
            pltpu.VMEM((2, 3 * depth, cols), F32),
            pltpu.VMEM((2, 3 * depth, cols), F32),
            pltpu.VMEM((2, rows, LANES), F32),
            pltpu.VMEM((2, 2 * depth, cols), F32),
            pltpu.VMEM((3, 2, 2 * LANES, cols), BF16),
            pltpu.VMEM((rows, 12 * ROWS), BF16),
            pltpu.VMEM((3, 4 * ROWS * planes, cols), F32),
            pltpu.VMEM((3, planes, rows, cols), F32),
            pltpu.VMEM((3 * cols, cols), BF16),
            dma((6,)), dma((3,)), dma, dma, dma, dma, dma, dma,
            dma((4,)), dma((4,)), dma((4,)), dma((4,)),
        ],
        compiler_params=pltpu.CompilerParams(
            collective_id=0, has_side_effects=True, vmem_limit_bytes=40 << 20
        ),
    )(*args)
    made = [pltpu.with_memory_space_constraint(x, pltpu.VMEM) for x in made]
    out = jax.ShapeDtypeStruct(shape, F32)
    return pl.pallas_call(
        update_kernel,
        out_shape=(out, out),
        in_specs=[pl.BlockSpec(memory_space=pltpu.VMEM)] * 6,
        out_specs=(pl.BlockSpec(memory_space=pltpu.HBM),) * 2,
        scratch_shapes=[pltpu.VMEM(shape, F32), pltpu.VMEM(shape, F32), dma((2,))],
        compiler_params=pltpu.CompilerParams(vmem_limit_bytes=20 << 20),
    )(*made)


def solution(mesh):
    brick = P(None, None, "gy", "gx")
    return jax.shard_map(
        functools.partial(body, mesh.shape["gx"], mesh.shape["gy"]),
        mesh=mesh,
        in_specs=(brick, brick, P(None, "gy", "gx", None), P(), P()),
        out_specs=(brick, brick),
        check_vma=False,
    )
```

```python
import functools
import math

import jax
import jax.numpy as jnp
from jax import lax
from jax.experimental import pallas as pl
from jax.experimental.pallas import tpu as pltpu
from jax.sharding import PartitionSpec as P

MESH = pl.DeviceIdType.MESH
F32 = jnp.float32
BF16 = jnp.bfloat16

R = 4
LANES = 128
ROWS = 8
UNROLL_BORDER = 8
UNROLL_BASE = 4
UNROLL_CROSS = 8
UNROLL_EDGE = 8
UNROLL_Z = 8
GROUP = 8
OUT = 4
TAIL = 16

alpha_pade = 0.25
coef_pade = 1.5
rk_keep = -5.0 / 9.0
rk_gain = 15.0 / 16.0
reynolds = 10000.0
decay = (-1.0 + math.sqrt(1.0 - 4.0 * alpha_pade * alpha_pade)) / (2.0 * alpha_pade)
scale = coef_pade / 2.0 * (1.0 + decay * decay)


def split(value):
    high = value.astype(BF16)
    low = (value - high.astype(F32)).astype(BF16)
    return high, low


def iota(shape, dim):
    return lax.broadcasted_iota(jnp.int32, shape, dim)


def tap_weights(taps, axis, offset, neighbour):
    out = jnp.zeros(offset.shape, F32)
    for o in range(R):
        for s in range(3):
            out = jnp.where((offset == o) & (neighbour == s), taps[axis, o, s], out)
    return out


def powers(shape, dim, flip):
    index = iota(shape, dim)
    if flip:
        index = shape[dim] - 1 - index
    magnitude = jnp.exp(index.astype(F32) * math.log(abs(decay)))
    return jnp.where((index & 1) == 1, -magnitude, magnitude)


def steps(count, unroll, body, carry):
    def outer(i, carry):
        for k in range(unroll):
            carry = body(i * unroll + k, carry)
        return carry

    return lax.fori_loop(0, count // unroll, outer, carry)


def difference(shape, dim_source, dim_target):
    step = iota(shape, dim_source) - iota(shape, dim_target)
    size = jnp.maximum(jnp.abs(step) - 1, 0)
    magnitude = jnp.exp(size.astype(F32) * math.log(abs(decay)))
    signed = jnp.where((size & 1) == 1, -magnitude, magnitude)
    return jnp.where(step > 0, signed, jnp.where(step < 0, -signed, 0.0))


def dot(a, b):
    return jnp.dot(a, b, preferred_element_type=F32)


def kernel(
    groups_x, groups_y, nu,
    taps_hbm, owner_hbm, mag_hbm, reg_hbm, vel_hbm,
    nm, nr, exr, eyr, ub, dy,
    taps, owner, vel, sv, s1, hs, rv, rh, bxs, bxr, bys, byr, exs, eys,
    px, py, xc, u, dx,
    in_sem, const_sem, vsend, vrecv, wsend, wrecv, hsend, hrecv, bsend, brecv, esend, erecv,
):
    gx, gy = lax.axis_index("gx"), lax.axis_index("gy")
    _, depth, rows, cols = nm.shape
    planes = groups_y

    vel_copy = pltpu.make_async_copy(vel_hbm, vel, const_sem.at[0])
    vel_copy.start()
    taps_copy = pltpu.make_async_copy(taps_hbm, taps, const_sem.at[1])
    owner_copy = pltpu.make_async_copy(owner_hbm, owner, const_sem.at[2])
    taps_copy.start()
    owner_copy.start()
    mag_copies, reg_copies = [], []
    for c in range(3):
        mag_copies.append(pltpu.make_async_copy(mag_hbm.at[c], nm.at[c], in_sem.at[c]))
        reg_copies.append(pltpu.make_async_copy(reg_hbm.at[c], nr.at[c], in_sem.at[3 + c]))
        mag_copies[c].start()
        reg_copies[c].start()

    barrier = pltpu.get_barrier_semaphore()
    x_low, x_high = lax.rem(gx + groups_x - 1, groups_x), lax.rem(gx + 1, groups_x)
    y_low, y_high = lax.rem(gy + groups_y - 1, groups_y), lax.rem(gy + 1, groups_y)
    sides = ((x_low, gy), (x_high, gy), (gx, y_low), (gx, y_high))
    far_x = sorted(range(1, groups_x), key=lambda i: abs(i - groups_x // 2))
    far_y = sorted(range(1, groups_y), key=lambda i: abs(i - groups_y // 2))
    for i in far_x:
        pl.semaphore_signal(
            barrier, inc=1, device_id=(lax.rem(gx + i, groups_x), gy), device_id_type=MESH
        )
    for i in far_y:
        pl.semaphore_signal(
            barrier, inc=1, device_id=(gx, lax.rem(gy + i, groups_y)), device_id_type=MESH
        )

    vel_copy.wait()
    half_lanes = LANES // 2
    lanes8 = iota((ROWS, LANES), 1)
    row8 = iota((ROWS, LANES), 0)
    tiles = vel.shape[3] // LANES
    flow = [[vel[c, 0, :, m * LANES : (m + 1) * LANES] for m in range(tiles)] for c in range(3)]
    for m in range(tiles):
        turned = [pltpu.roll(flow[c][m], half_lanes, 1) for c in range(3)]
        for odd in range(2):
            first, second, third = (
                (turned[0], flow[1][m], turned[2]) if odd else (flow[0][m], turned[1], flow[2][m])
            )
            sv[2 * m + odd, 0] = jnp.where(lanes8 < half_lanes, first, second)
            tile = jnp.where(lanes8 < half_lanes, third, 0.0)
            for c in range(3):
                if odd:
                    below = flow[c][m][:, half_lanes - 1 : half_lanes]
                    above = flow[c][(m + 1) % tiles][:, 0:1]
                else:
                    below = flow[c][(m - 1) % tiles][:, LANES - 1 : LANES]
                    above = flow[c][m][:, half_lanes : half_lanes + 1]
                tile = jnp.where(lanes8 == half_lanes + c, below, tile)
                tile = jnp.where(lanes8 == half_lanes + 3 + c, above, tile)
            sv[2 * m + odd, 1] = tile
    s1[gx] = sv[gx]

    pl.semaphore_wait(barrier, groups_x + groups_y - 2)

    for i in far_x:
        t = lax.rem(gx + i, groups_x)
        pltpu.make_async_remote_copy(
            src_ref=sv.at[t], dst_ref=s1.at[gx], send_sem=vsend, recv_sem=vrecv,
            device_id=(t, gy), device_id_type=MESH,
        ).start()

    taps_copy.wait()
    owner_copy.wait()
    shape = (2 * LANES, cols)
    q, f = iota(shape, 0), iota(shape, 1)
    for c in range(3):
        place = q - c * half_lanes
        place = jnp.where((place >= 0) & (place < half_lanes), place, -100)
        place = jnp.where(q == 3 * half_lanes + c, -1, place)
        place = jnp.where(q == 3 * half_lanes + 3 + c, half_lanes, place)
        px[c, 0], px[c, 1] = split(tap_weights(taps, 0, f & 3, place - (f >> 2) + 1))
    shape = (rows, 12 * ROWS)
    f, q = iota(shape, 0), iota(shape, 1)
    third_part = q >= 8 * ROWS
    q = q & (4 * ROWS - 1)
    place = jnp.where(q < 2 * ROWS, q, -100)
    place = jnp.where((q == 2 * ROWS) | (q == 3 * ROWS + 2), -1, place)
    place = jnp.where((q == 2 * ROWS + 1) | (q == 3 * ROWS + 3), 2 * ROWS, place)
    weights = tap_weights(taps, 1, f & 3, place - (f >> 2) + 1) * (scale * 0.25)
    high = weights.astype(BF16).astype(F32)
    py[...] = jnp.where(third_part, weights - high, high).astype(BF16)
    high, low = split(difference((cols, cols), 0, 1))
    dx[0:cols, :] = high
    dx[cols : 2 * cols, :] = high
    dx[2 * cols : 3 * cols, :] = low
    high, low = split(difference((rows, rows), 1, 0))
    dy[...] = jnp.concatenate([high.astype(F32), high.astype(F32), low.astype(F32)], axis=1).astype(BF16)

    row_of = iota((rows, cols), 0)
    lane_of = iota((rows, cols), 1)
    edge_lane = iota((rows, LANES), 1)

    def base_of(c):
        reg_copies[c].wait()

        def base(z, _):
            b = nm[c, z]
            before = nm[c, lax.rem(z + depth - 1, depth)]
            after = nm[c, lax.rem(z + 1, depth)]
            total = before + after - 6.0 * b
            total = total + jnp.where(row_of == 0, 0.0, pltpu.roll(b, 1, 0))
            total = total + jnp.where(row_of == rows - 1, 0.0, pltpu.roll(b, rows - 1, 0))
            total = total + jnp.where(lane_of == 0, 0.0, pltpu.roll(b, 1, 1))
            total = total + jnp.where(lane_of == cols - 1, 0.0, pltpu.roll(b, cols - 1, 1))
            nr[c, z] = rk_keep * nr[c, z] + nu * total
            return 0

        steps(depth, UNROLL_BASE, base, 0)

    def exchange(xs, xr, ys, yr, ssem, rsem, which=(2, 3, 0, 1)):
        copies = []
        for k in which:
            src, dst = (xs, xr) if k < 2 else (ys, yr)
            copies.append(
                pltpu.make_async_remote_copy(
                    src_ref=src.at[k % 2], dst_ref=dst.at[1 - k % 2],
                    send_sem=ssem.at[k], recv_sem=rsem.at[k],
                    device_id=sides[k], device_id_type=MESH,
                )
            )
            copies[-1].start()
        return copies

    edges = (jnp.zeros((rows, LANES), F32), jnp.zeros((rows, LANES), F32))
    for c in range(3):
        mag_copies[c].wait()

        def border(z, carry):
            low, high = carry
            bys[0, pl.ds(c * depth + z, 1), :] = nm[c, z, 0:1, :]
            bys[1, pl.ds(c * depth + z, 1), :] = nm[c, z, rows - 1 : rows, :]
            here = edge_lane == c * 32 + z
            low = jnp.where(here, nm[c, z, :, 0:1], low)
            high = jnp.where(here, nm[c, z, :, cols - 1 : cols], high)
            return low, high

        edges = steps(depth, UNROLL_BORDER, border, edges)
    bxs[0], bxs[1] = edges

    base_of(0)

    others = s1.at[pl.ds(0, groups_x - 1)]
    pltpu.make_async_copy(others, others, vrecv).wait()
    for g in range(groups_y):
        below, above = (2 * g - 1) % groups_x, (2 * g + 2) % groups_x
        tile = jnp.zeros((ROWS, LANES), F32)
        for k in range(2):
            tile = jnp.where(row8 == 2 * k, s1[below, k, ROWS - 1 : ROWS, :], tile)
            tile = jnp.where(row8 == 2 * k + 1, s1[above, k, 0:1, :], tile)
        hs[g] = tile
    rv[gy] = s1[pl.ds(2 * gy, 2)]
    rh[gy] = hs[gy]

    for i in far_y:
        g = lax.rem(gy + i, groups_y)
        pltpu.make_async_remote_copy(
            src_ref=s1.at[pl.ds(2 * g, 2)], dst_ref=rv.at[gy], send_sem=wsend, recv_sem=wrecv,
            device_id=(gx, g), device_id_type=MESH,
        ).start()
        pltpu.make_async_remote_copy(
            src_ref=hs.at[g], dst_ref=rh.at[gy], send_sem=hsend, recv_sem=hrecv,
            device_id=(gx, g), device_id_type=MESH,
        ).start()

    b_copies = exchange(bxs, bxr, bys, byr, bsend, brecv)
    base_of(1)
    base_of(2)

    others = rv.at[pl.ds(0, planes - 1)]
    pltpu.make_async_copy(others, others, wrecv).wait()
    others = rh.at[pl.ds(0, planes - 1)]
    pltpu.make_async_copy(others, others, hrecv).wait()
    main = 2 * ROWS * planes
    blocks = [rv[:, :, k].reshape(main, LANES) for k in range(2)]
    beside = rh[...].reshape(ROWS * planes, LANES)
    blank = jnp.zeros_like(beside)
    coarse = jnp.concatenate(
        [
            jnp.concatenate(blocks, axis=1),
            jnp.concatenate([beside, blank], axis=1),
            jnp.concatenate([blank, beside], axis=1),
        ],
        axis=0,
    )
    high, low = split(coarse)
    for c in range(3):
        xc[c] = dot(high, px[c, 0]) + dot(low, px[c, 0]) + dot(high, px[c, 1])
    for p in range(planes):
        for c in range(3):
            a0 = main + p * ROWS
            b0 = a0 + planes * ROWS
            near = jnp.concatenate(
                [
                    xc[c, p * 2 * ROWS : (p + 1) * 2 * ROWS, :],
                    xc[c, a0 : a0 + ROWS, :],
                    xc[c, b0 : b0 + ROWS, :],
                ],
                axis=0,
            )
            high, low = split(near)
            u[c, p] = dot(py[...], jnp.concatenate([high, low, high], axis=0))

    strip = 2 * ROWS
    lane_low = powers((1, LANES), 1, False)
    lane_high = powers((1, LANES), 1, True)
    sub_low = powers((strip, cols), 0, False)
    sub_high = powers((strip, cols), 0, True)
    weights_z = [[taps[2, o, n] for n in range(3)] for o in range(R)]

    def stored(p):
        at = jnp.int32(0)
        for b in range(planes):
            at = jnp.where(owner[b] == p, b, at)
        return at

    def strips(j, _):
        part = pl.ds(pl.multiple_of(j * ROWS, ROWS), ROWS)

        def cross(p, carry):
            low, high = carry
            around = [stored(lax.rem(p + planes + n - 1, planes)) for n in range(3)]
            near = [[u[c, around[n], part, :] for n in range(3)] for c in range(3)]
            for o in range(R):
                z = p * R + o
                us = []
                for c in range(3):
                    total = weights_z[o][0] * near[c][0] + weights_z[o][1] * near[c][1]
                    us.append(total + weights_z[o][2] * near[c][2])
                bs = [nm[c, z, part, :] for c in range(3)]
                for c in range(3):
                    a, b = (c + 1) % 3, (c + 2) % 3
                    e = us[a] * bs[b] - us[b] * bs[a]
                    ub[c, z, part, :] = e
                    if c > 0:
                        here = lanes8 == (c - 1) * 32 + z
                        sum_low = jnp.sum(e[:, :LANES] * lane_low, axis=1, keepdims=True)
                        sum_high = jnp.sum(e[:, cols - LANES :] * lane_high, axis=1, keepdims=True)
                        low = jnp.where(here, sum_low, low)
                        high = jnp.where(here, sum_high, high)
            return low, high

        zeros = jnp.zeros((ROWS, LANES), F32)
        low, high = steps(planes, UNROLL_CROSS, cross, (zeros, zeros))
        exs[0, part, :] = low
        exs[1, part, :] = high
        return 0

    count = rows // ROWS
    lax.fori_loop(0, 4, lambda k, _: strips(k + (count - 4) * (k // 2), 0), 0)

    def edge(z, _):
        for k, c in enumerate((0, 2)):
            at = pl.ds(k * depth + z, 1)
            eys[0, at, :] = jnp.sum(ub[c, z, 0:strip, :] * sub_low, axis=0, keepdims=True)
            eys[1, at, :] = jnp.sum(ub[c, z, rows - strip : rows, :] * sub_high, axis=0, keepdims=True)
        return 0

    steps(depth, UNROLL_EDGE, edge, 0)
    e_copies = exchange(exs, exr, eys, eyr, esend, erecv, (2, 3))
    lax.fori_loop(2, count - 2, strips, 0)
    e_copies = e_copies + exchange(exs, exr, eys, eyr, esend, erecv, (0, 1))

    warm = TAIL if depth > TAIL else depth
    wrap = 1.0 if depth > TAIL else 1.0 / (1.0 - decay**depth)

    def strips_z(j, _):
        r0 = pl.multiple_of(j * strip, strip)
        part = pl.ds(r0, strip)

        def warm_up(i, carry):
            bx, by, ax, ay = carry
            z = depth - warm + i
            bx = ub[0, z, part, :] + decay * bx
            by = ub[1, z, part, :] + decay * by
            z = warm - 1 - i
            ax = ub[0, z, part, :] + decay * ax
            ay = ub[1, z, part, :] + decay * ay
            return bx, by, ax, ay

        zeros = jnp.zeros((strip, cols), F32)
        carry = steps(warm, UNROLL_Z, warm_up, (zeros,) * 4)
        if wrap != 1.0:
            carry = tuple(wrap * value for value in carry)

        def along_z(i, carry):
            bx, by, ax, ay = carry
            z = i
            nr[1, z, part, :] += -bx
            nr[0, z, part, :] += by
            bx = ub[0, z, part, :] + decay * bx
            by = ub[1, z, part, :] + decay * by
            z = depth - 1 - i
            nr[1, z, part, :] += ax
            nr[0, z, part, :] += -ay
            ax = ub[0, z, part, :] + decay * ax
            ay = ub[1, z, part, :] + decay * ay
            return bx, by, ax, ay

        steps(depth, UNROLL_Z, along_z, carry)
        return 0

    lax.fori_loop(0, rows // strip, strips_z, 0)

    first_row = jnp.where(iota((ROWS, cols), 0) == 0, nu, 0.0)
    last_row = jnp.where(iota((ROWS, cols), 0) == ROWS - 1, nu, 0.0)
    first_lane = jnp.where(iota((1, LANES), 1) == 0, nu, 0.0)
    last_lane = jnp.where(iota((1, LANES), 1) == LANES - 1, nu, 0.0)
    for copy in b_copies:
        copy.wait_recv()

    def group(i, _):
        at = pl.ds(i * GROUP, GROUP)
        back = lax.rem(LANES - i * GROUP, LANES)
        near = [pltpu.roll(bxr[k], back, 1) for k in range(2)]
        along_x = []
        for c in (1, 2):
            high, low = split(ub[c, at].reshape(GROUP * rows, cols))
            out = dot(jnp.concatenate([high, low, high], axis=1), dx[...])
            along_x.append(out.reshape(GROUP, rows, cols))
        for k in range(GROUP):
            z = i * GROUP + k
            for c in range(3):
                spot = c * 32 + k
                lo = near[0][:, spot : spot + 1] * first_lane
                hi = near[1][:, spot : spot + 1] * last_lane
                total = nr[c, z] + jnp.concatenate([lo, hi], axis=1)
                if c == 1:
                    total = total - along_x[1][k]
                if c == 2:
                    total = total + along_x[0][k]
                top = byr[0, pl.ds(c * depth + z, 1), :] * first_row
                bottom = byr[1, pl.ds(c * depth + z, 1), :] * last_row
                nr[c, z] = jnp.concatenate(
                    [total[:ROWS] + top, total[ROWS : rows - ROWS], total[rows - ROWS :] + bottom], axis=0
                )
        return 0

    lax.fori_loop(0, depth // GROUP, group, 0)

    for copy in e_copies:
        copy.wait_recv()
    for copy in b_copies + e_copies:
        copy.wait_send()
    for ref, sem, count in ((sv, vsend, groups_x), (rv, wsend, groups_y), (rh, hsend, groups_y)):
        part = ref.at[pl.ds(0, count - 1)]
        pltpu.make_async_copy(part, part, sem).wait()


def update_kernel(b, partial, exr, eyr, ub, dy, mag_hbm, reg_hbm, nm, nr, sems):
    _, depth, rows, cols = b.shape
    strip = 2 * ROWS
    lane_low = powers((1, LANES), 1, False)
    lane_high = powers((1, LANES), 1, True)
    sub_low = powers((strip, cols), 0, False)
    sub_high = powers((strip, cols), 0, True)

    def planes(i, _):
        back = lax.rem(LANES - i * OUT, LANES)
        near = [pltpu.roll(exr[k], back, 1) for k in range(2)]
        for k in range(OUT):
            z = i * OUT + k
            for c in range(3):
                total = partial[c, z]
                if c != 1:
                    high, low = split(ub[2 - c, z])
                    out = dot(dy[...], jnp.concatenate([high, low, high], axis=0))
                    total = total + out if c == 0 else total - out
                if c == 1:
                    lo = near[0][:, 32 + k : 33 + k] * lane_low
                    hi = near[1][:, 32 + k : 33 + k] * lane_high
                    total = total + jnp.concatenate([lo, -hi], axis=1)
                if c == 2:
                    lo = near[0][:, k : k + 1] * lane_low
                    hi = near[1][:, k : k + 1] * lane_high
                    total = total - jnp.concatenate([lo, -hi], axis=1)
                if c != 1:
                    at = pl.ds(z if c == 2 else depth + z, 1)
                    top = eyr[0, at, :] * sub_low
                    bottom = eyr[1, at, :] * sub_high
                    first, last = total[:strip], total[rows - strip :]
                    first, last = (first - top, last + bottom) if c == 0 else (first + top, last - bottom)
                    total = jnp.concatenate([first, total[strip : rows - strip], last], axis=0)
                nr[c, z] = total
                nm[c, z] = b[c, z] + rk_gain * total
        at = pl.ds(i * OUT, OUT)
        for c in range(3):
            pltpu.make_async_copy(nr.at[c, at], reg_hbm.at[c, at], sems.at[0]).start()
            pltpu.make_async_copy(nm.at[c, at], mag_hbm.at[c, at], sems.at[1]).start()
        return 0

    lax.fori_loop(0, depth // OUT, planes, 0)
    pltpu.make_async_copy(nr, reg_hbm, sems.at[0]).wait()
    pltpu.make_async_copy(nm, mag_hbm, sems.at[1]).wait()


def body(groups_x, groups_y, magnetic, register, velocity, prolong_taps, owner_map):
    shape = magnetic.shape
    _, depth, rows, cols = shape
    planes = groups_y
    spacing = 2.0 * math.pi / (cols * groups_x)
    nu = 2.0 * math.pi / reynolds / (4.0 * spacing)
    brick = pltpu.VMEM(shape, F32)
    dma = pltpu.SemaphoreType.DMA
    args = [
        pltpu.with_memory_space_constraint(x, pltpu.HBM)
        for x in (prolong_taps, owner_map, magnetic, register, velocity)
    ]
    made = pl.pallas_call(
        functools.partial(kernel, groups_x, groups_y, nu),
        out_shape=(
            brick, brick, pltpu.VMEM((2, rows, LANES), F32), pltpu.VMEM((2, 2 * depth, cols), F32),
            brick, pltpu.VMEM((rows, 3 * rows), BF16),
        ),
        in_specs=[pl.BlockSpec(memory_space=pltpu.HBM)] * 5,
        out_specs=(pl.BlockSpec(memory_space=pltpu.VMEM),) * 6,
        scratch_shapes=[
            pltpu.SMEM(prolong_taps.shape, F32),
            pltpu.SMEM(owner_map.shape, jnp.int32),
            pltpu.VMEM(velocity.shape, F32),
            pltpu.VMEM((groups_x, 2, ROWS, LANES), F32),
            pltpu.VMEM((groups_x, 2, ROWS, LANES), F32),
            pltpu.VMEM((groups_y, ROWS, LANES), F32),
            pltpu.VMEM((planes, 2, 2, ROWS, LANES), F32),
            pltpu.VMEM((planes, ROWS, LANES), F32),
            pltpu.VMEM((2, rows, LANES), F32),
            pltpu.VMEM((2, rows, LANES), F32),
            pltpu.VMEM((2, 3 * depth, cols), F32),
            pltpu.VMEM((2, 3 * depth, cols), F32),
            pltpu.VMEM((2, rows, LANES), F32),
            pltpu.VMEM((2, 2 * depth, cols), F32),
            pltpu.VMEM((3, 2, 2 * LANES, cols), BF16),
            pltpu.VMEM((rows, 12 * ROWS), BF16),
            pltpu.VMEM((3, 4 * ROWS * planes, cols), F32),
            pltpu.VMEM((3, planes, rows, cols), F32),
            pltpu.VMEM((3 * cols, cols), BF16),
            dma((6,)), dma((3,)), dma, dma, dma, dma, dma, dma,
            dma((4,)), dma((4,)), dma((4,)), dma((4,)),
        ],
        compiler_params=pltpu.CompilerParams(
            collective_id=0, has_side_effects=True, vmem_limit_bytes=40 << 20
        ),
    )(*args)
    made = [pltpu.with_memory_space_constraint(x, pltpu.VMEM) for x in made]
    out = jax.ShapeDtypeStruct(shape, F32)
    return pl.pallas_call(
        update_kernel,
        out_shape=(out, out),
        in_specs=[pl.BlockSpec(memory_space=pltpu.VMEM)] * 6,
        out_specs=(pl.BlockSpec(memory_space=pltpu.HBM),) * 2,
        scratch_shapes=[pltpu.VMEM(shape, F32), pltpu.VMEM(shape, F32), dma((2,))],
        compiler_params=pltpu.CompilerParams(vmem_limit_bytes=20 << 20),
    )(*made)


def solution(mesh):
    brick = P(None, None, "gy", "gx")
    return jax.shard_map(
        functools.partial(body, mesh.shape["gx"], mesh.shape["gy"]),
        mesh=mesh,
        in_specs=(brick, brick, P(None, "gy", "gx", None), P(), P()),
        out_specs=(brick, brick),
        check_vma=False,
    )
```
